128 devices in a mesh: grp: 4 (over y_lo, core), slab: 32 (over z, x, y_hi).
Axes of the slice: x: 4, y: 4 (y_hi: 2, y_lo: 2; y = y_hi * 2 + y_lo), z: 4, core: 2. Of those that a mesh axis runs over, the one named last changes fastest.
Arguments:
- modes: bfloat16 [512, 2, 384, 384], P(('grp', 'slab')), may hold values from -0.21875 to 0.21875
- occup: float32 [512, 384], P(('grp', 'slab')), may hold values from 0.2 to 5
- qprime_coord: int32 [3, 512], P(None, ('grp', 'slab')), may hold values from 0 to 15
- shell_vec: int32 [3, 128], replicated, may hold values from -3 to 3
- target_coord: int32 [3, 128], replicated, may hold values from 0 to 15
- pair_atoms: int32 [2, 1024], replicated, may hold values from 0 to 127
- block_in: int32 [2097152], P(('grp', 'slab')), may hold values from 0 to 4095
- block_out: int32 [2097152], P(('grp', 'slab')), may hold values from 0 to 4095
- fc4: bfloat16 [81, 2097152], P(None, ('grp', 'slab')), may hold values from -0.29882812 to 0.29882812
Outputs:
- delta: float32 [128, 2, 9, 1024], P(('grp', 'slab'))
The draws below stay inside these ranges and needn't reach their ends.
All inputs are finite; a program needn't handle non-finite values.
Results may differ from the reference program's by a relative error of at most 0.0024.
Values sent between devices are 32-bit elements; how exact they have to be, the bound alone decides.
No kernel may reach another device: no remote copies, remote signals or barrier semaphores. Data moves between devices by JAX's collectives and lax.ppermute only.
A program may use at most 256 MiB of HBM per device.

```python
import math
import jax
import jax.numpy as jnp
from jax import lax

NA = 128
B = 384
MESH = 16
P_SIZE = 1024
SH = 4
K_DEV = 16384
NR = 128
QP = 512
QT = 128
KTOT = 2097152
N_GRP = 4
N_SLAB = 32


def plant(values, rng, smallest, high):
    shape = values.shape
    index_at = [jax.random.randint(jax.random.fold_in(rng, axis), (), 0, shape[axis]) for axis in range(len(shape))]
    values = values.at[tuple(index_at)].set(smallest)
    longest = shape.index(max(shape))
    index_at[longest] = (index_at[longest] + 1) % shape[longest]
    return values.at[tuple(index_at)].set(high)


def level_of(key, shape, cuts, low, largest):
    factor_of = 1.0
    for dim, blocks in cuts:
        heights = jax.random.uniform(jax.random.fold_in(jax.random.fold_in(key, 6), dim), (blocks,), jnp.float32, low / len(cuts), largest / len(cuts))
        factor_of = factor_of * jnp.repeat(jnp.exp(heights), shape[dim] // blocks).reshape((-1,) + (1,) * (len(shape) - 1 - dim))
    return factor_of


def bell_draw(stream_key, shape, deviation, reach, shards=(), dtype=jnp.bfloat16):
    values = deviation * jax.random.normal(stream_key, shape, jnp.float32)
    if shards:
        values = values * level_of(stream_key, shape, shards, -0.22, 0.18)
    return jnp.clip(values, -reach, reach).astype(dtype)


def setup_inputs(seed: int = 0) -> dict:
    streams_of = jax.random.split(jax.random.key(seed), 10)
    return {
        "modes": bell_draw(streams_of[0], (QP, 2, B, B), (2 * B) ** -0.5, 0.21875, ((0, 128),)),
        "occup": jnp.clip(jnp.exp(math.log(5.0) - 3.218876 * jax.random.uniform(streams_of[1], (QP, B), jnp.float32) ** level_of(streams_of[1], (QP, B), ((0, 128),), -0.2, 0.2)), 0.2, 5.0),
        "qprime_coord": plant(jax.random.randint(streams_of[2], (3, QP), 0, MESH), jax.random.fold_in(streams_of[2], 1), 0, MESH - 1).astype(jnp.int32),
        "shell_vec": plant(jax.random.randint(streams_of[3], (3, NR), -3, 4), jax.random.fold_in(streams_of[3], 1), -3, 3).astype(jnp.int32),
        "target_coord": plant(jax.random.randint(streams_of[4], (3, QT), 0, MESH), jax.random.fold_in(streams_of[4], 1), 0, MESH - 1).astype(jnp.int32),
        "pair_atoms": plant(jax.random.randint(streams_of[5], (2, P_SIZE), 0, NA), jax.random.fold_in(streams_of[5], 1), 0, NA - 1).astype(jnp.int32),
        "block_in": plant(jax.random.randint(streams_of[6], (KTOT,), 0, SH * P_SIZE), jax.random.fold_in(streams_of[6], 1), 0, (SH * P_SIZE) - 1).astype(jnp.int32),
        "block_out": plant(jax.random.randint(streams_of[7], (KTOT,), 0, SH * P_SIZE), jax.random.fold_in(streams_of[7], 1), 0, (SH * P_SIZE) - 1).astype(jnp.int32),
        "fc4": bell_draw(streams_of[8], (81, KTOT), 0.05, 0.29882812, ((1, 128),)),
    }


def phases(coords, shells):
    wave_index = jnp.mod(lax.optimization_barrier(jnp.sum(coords[:, :, None] * shells[:, None, :], axis=0)), MESH)
    angle = 2.0 * math.pi / MESH * wave_index.astype(jnp.float32)
    return (jnp.cos(angle), jnp.sin(angle))

def pair_density(mode_pair, weights, atom_first, atom_second):
    real_part = mode_pair[0]
    imag_part = mode_pair[1]
    left_rows = jnp.concatenate([real_part, imag_part], 1)
    doubled = jnp.concatenate([weights, weights])
    scaled = (left_rows.astype(jnp.float32) * doubled[None, :]).astype(jnp.bfloat16)
    right_rows = jnp.concatenate([left_rows, jnp.concatenate([imag_part, -real_part], 1)], 0)
    density = jnp.dot(right_rows, scaled.T, preferred_element_type=jnp.float32)
    natoms = real_part.shape[0] // 3
    blocked = density.reshape(2, natoms, 3, natoms, 3).transpose(1, 3, 0, 2, 4)
    picked = blocked[atom_first, atom_second]
    return picked.reshape(atom_first.shape[0], 2, 9).transpose(1, 2, 0)

def reference(modes, occup, qprime_coord, shell_vec, target_coord, pair_atoms, block_in, block_out, fc4):
    cos_prime, sin_prime = phases(qprime_coord, shell_vec)
    atom_first = pair_atoms[0]
    atom_second = pair_atoms[1]

    def add_point(running, inputs):
        mode_pair, weights, cos_row, sin_row = inputs
        pieces = pair_density(mode_pair, weights, atom_first, atom_second)
        running = running + cos_row[:, None, None] * pieces[0][None] - sin_row[:, None, None] * pieces[1][None]
        return (running, None)
    running = lax.scan(add_point, jnp.zeros((NR, 9, P_SIZE), jnp.float32), (modes, occup, cos_prime, sin_prime))[0]
    rho = running / math.sqrt(QP)
    rho_rows = rho.transpose(1, 0, 2).reshape(9, NR * P_SIZE)
    ndevices = N_GRP * N_SLAB

    def add_device(device, renorm):
        coeffs = lax.dynamic_slice_in_dim(fc4, device * K_DEV, K_DEV, 1).astype(jnp.float32)
        reads = lax.dynamic_slice_in_dim(block_in, device * K_DEV, K_DEV, 0)
        writes = lax.dynamic_slice_in_dim(block_out, device * K_DEV, K_DEV, 0)
        shell_start = (jnp.mod(device, N_SLAB) * SH * P_SIZE).astype(jnp.int32)
        gathered = rho_rows[:, reads + shell_start]
        contrib = lax.optimization_barrier(jnp.sum(coeffs.reshape(9, 9, K_DEV) * gathered[None], axis=1))
        return renorm.at[:, writes + shell_start].add(contrib)
    renorm = lax.fori_loop(0, ndevices, add_device, jnp.zeros((9, NR * P_SIZE), jnp.float32))
    shell_rows = renorm.reshape(9, NR, P_SIZE).transpose(1, 0, 2).reshape(NR, 9 * P_SIZE)
    cos_target, sin_target = phases(target_coord, shell_vec)
    real_out = jnp.dot(cos_target, shell_rows, precision=lax.Precision.HIGHEST)
    imag_out = -jnp.dot(sin_target, shell_rows, precision=lax.Precision.HIGHEST)
    return jnp.stack([real_out, imag_out], 1).reshape(QT, 2, 9, P_SIZE)
```

```python
import math

import jax
import jax.numpy as jnp
import numpy as np
from jax import lax
from jax.experimental import pallas as pl
from jax.experimental.pallas import tpu as pltpu
from jax.sharding import PartitionSpec as P

MESH = 16
LANES = 128
NDEV = 128
NPH = 8
COLS = 72
MSG = 75
ALL = ("grp", "slab")
F32 = jnp.float32
BF16 = jnp.bfloat16
HIGHEST = lax.Precision.HIGHEST
VMEM_LIMIT = 48 * 1024 * 1024


def params():
    return pltpu.CompilerParams(vmem_limit_bytes=VMEM_LIMIT)


def sixteenth_cos(index):
    wrapped = index - 16.0 * jnp.floor(index * (1.0 / 16.0))
    folded = 4.0 - jnp.minimum(wrapped, 16.0 - wrapped)
    square = folded * folded
    poly = POLY[3]
    for coefficient in (POLY[2], POLY[1], POLY[0]):
        poly = poly * square + coefficient
    return folded * poly


def odd_polynomial():
    points = np.arange(1, 5, dtype=np.float64)
    values = np.sin(np.pi * points / 8.0)
    powers = np.stack([points ** (2 * k + 1) for k in range(4)], 1)
    return [float(c) for c in np.linalg.solve(powers, values)]


POLY = odd_polynomial()


def pick_body(
    coord, atoms, modes, occup, out, held, weights, pairs, spots, points, scaled, rows, dens, sems
):
    copies = [
        pltpu.make_async_copy(occup, weights, sems.at[4]),
        pltpu.make_async_copy(atoms, pairs, sems.at[5]),
        pltpu.make_async_copy(coord, points, sems.at[6]),
    ]
    loads = [pltpu.make_async_copy(modes.at[q], held.at[q], sems.at[q]) for q in range(4)]
    loads[0].start()
    for copy in copies:
        copy.start()
    for load in loads[1:]:
        load.start()
    copies[1].wait()
    first = pairs[0:1, :]
    second = pairs[1:2, :]
    turn = (128 - 3 * (first & 31)) & 127
    pairs[0:1, :] = ((first >> 5) * 3072 + second * 24) * 128 + turn
    move = pltpu.make_async_copy(pairs.at[0], spots, sems.at[7])
    move.start()
    copies[0].wait()
    for q in range(4):
        loads[q].wait()
        weight = weights[q : q + 1, :]
        for part in range(2):
            values = held[q, part]
            span = pl.ds(384 * part, 384)
            scaled[:, span] = (values.astype(F32) * weight).astype(BF16)
            for block in range(4):
                piece = values[96 * block : 96 * block + 96]
                rows[128 * block : 128 * block + 96, span] = piece
                other = piece if part == 1 else -piece
                low = 512 + 128 * block
                rows[low : low + 96, pl.ds(384 * (1 - part), 384)] = other
        for comp in range(2):
            for half in range(2):
                start = 512 * comp + 256 * half
                tile = lax.dot_general(
                    scaled[...],
                    rows[start : start + 256],
                    (((1,), (1,)), ((), ())),
                    preferred_element_type=F32,
                )
                for low in range(2):
                    base = 3072 * (2 * half + low) + 2 * q + comp
                    dens[pl.ds(base, 384, stride=8), :] = tile[:, 128 * low : 128 * low + 128]

    lane = lax.broadcasted_iota(jnp.int32, (8, LANES), 1)
    row = lax.broadcasted_iota(jnp.int32, (8, LANES), 0)
    copies[2].wait()
    move.wait()
    start = jnp.zeros((8, LANES), F32)
    for q in range(4):
        for axis in range(3):
            here = (row // 2 == q) & (lane == COLS + axis)
            start = jnp.where(here, points[axis, q].astype(F32), start)

    def one(dev, carry):
        acc = start
        for high in range(NPH):
            spot = spots[high * LANES + dev]
            base = spot >> 7
            for beta in range(3):
                low = 24 * beta + 3 * high
                value = dens[pl.ds(pl.multiple_of(base + 8 * beta, 8), 8), :]
                turned = pltpu.roll(value, (spot + low) & 127, 1)
                acc = jnp.where((lane >= low) & (lane < low + 3), turned, acc)
        out[dev] = acc[:, :MSG]
        return carry

    lax.fori_loop(0, NDEV, one, 0, unroll=16)


def pick(modes, occup, coord, atoms):
    anywhere = pl.BlockSpec(memory_space=pl.ANY)
    return pl.pallas_call(
        pick_body,
        in_specs=[anywhere] * 4,
        out_specs=pl.BlockSpec(memory_space=pltpu.VMEM),
        out_shape=jax.ShapeDtypeStruct((NDEV, 8, MSG), F32),
        scratch_shapes=[
            pltpu.VMEM((4, 2, 384, 384), BF16),
            pltpu.VMEM((4, 384), F32),
            pltpu.VMEM((2, NPH * LANES), jnp.int32),
            pltpu.SMEM((NPH * LANES,), jnp.int32),
            pltpu.SMEM((3, 4), jnp.int32),
            pltpu.VMEM((384, 768), BF16),
            pltpu.VMEM((1024, 768), BF16),
            pltpu.VMEM((4 * 384 * 8, LANES), F32),
            pltpu.SemaphoreType.DMA((8,)),
        ],
        compiler_params=params(),
    )(coord, atoms, modes, occup)


def shells_body(received, shell, out):
    values = received[...].reshape(NDEV * 8, MSG)
    vectors = jnp.concatenate([jnp.zeros((COLS, LANES), F32), shell[...].astype(F32)], 0)
    index = lax.dot_general(
        vectors, values, (((0,), (1,)), ((), ())), preferred_element_type=F32
    )
    lane = lax.broadcasted_iota(jnp.int32, index.shape, 1)
    index = index + jnp.where(lane % 2 == 1, 4.0, 0.0)
    rho = jnp.dot(sixteenth_cos(index), values, precision=HIGHEST, preferred_element_type=F32)
    rho = rho[:, :COLS] * (1.0 / math.sqrt(512.0))
    for slab in range(32):
        piece = rho[4 * slab : 4 * slab + 4]
        for group in range(4):
            out[32 * group + slab] = piece


def to_shells(received, shell):
    return pl.pallas_call(
        shells_body,
        out_shape=jax.ShapeDtypeStruct((NDEV, 4, COLS), F32),
        compiler_params=params(),
    )(received, shell)


def block_tables():
    row = np.arange(2 * COLS)
    column = row % COLS
    beta, high, alpha = column // 24, (column % 24) // 3, column % 3
    comp = 3 * alpha + beta
    level = 8 * (row // COLS) + high
    term = np.arange(81)
    repeat = (term[:, None] % 9 == comp[None, :]).astype(np.float32)
    collect = (comp[:, None] == term[None, :] // 9).astype(np.float32)
    return repeat, collect, level.astype(np.int32)[:, None]


def contract_body(chunk, unroll, received, repeat, collect, level, reads, writes, fc4, out, table, total):
    for shell in range(4):
        piece = received[:, shell, :]
        piece = jnp.concatenate([piece, jnp.zeros((NDEV, LANES - COLS), F32)], 1)
        low, high = shell % 2, shell // 2
        table[low * COLS : low * COLS + COLS, high * LANES : high * LANES + LANES] = piece.T[
            :COLS
        ].astype(BF16)
    total[...] = jnp.zeros_like(total)
    place = lax.broadcasted_iota(jnp.int32, (2 * LANES, chunk), 0)

    def split(entry):
        low = ((entry >> 11) << 7) | (entry & 127)
        return jnp.where(place == low, 1.0, 0.0).astype(BF16), (entry >> 7) & 15

    def one(step, carry):
        span = pl.ds(pl.multiple_of(step * chunk, chunk), chunk)
        read_low, read_high = split(reads[:, span])
        write_low, write_high = split(writes[:, span])
        found = jnp.dot(table[...], read_low, preferred_element_type=F32)
        found = jnp.where(level[...] == read_high, found, 0.0).astype(BF16)
        spread = jnp.dot(repeat[...], found, preferred_element_type=F32)
        product = fc4[:, span].astype(F32) * spread
        coarse = product.astype(BF16)
        fine = (product - coarse.astype(F32)).astype(BF16)
        contrib = jnp.dot(collect[...], coarse, preferred_element_type=F32)
        contrib = contrib + jnp.dot(collect[...], fine, preferred_element_type=F32)
        contrib = jnp.where(level[...] == write_high, contrib, 0.0)
        coarse = contrib.astype(BF16)
        fine = (contrib - coarse.astype(F32)).astype(BF16)
        total[...] += lax.dot_general(
            jnp.concatenate([coarse, fine], 0),
            write_low,
            (((1,), (1,)), ((), ())),
            preferred_element_type=F32,
        )
        return carry

    lax.fori_loop(0, fc4.shape[1] // chunk, one, 0, unroll=unroll)
    for shell in range(4):
        low, high = shell % 2, shell // 2
        span = pl.ds(high * LANES, LANES)
        piece = total[low * COLS : low * COLS + COLS, span]
        piece = piece + total[(2 + low) * COLS : (2 + low) * COLS + COLS, span]
        piece = jnp.concatenate([piece, jnp.zeros((LANES - COLS, LANES), F32)], 0)
        out[:, shell, :] = piece.T[:, :COLS]


def contract(received, block_in, block_out, fc4, chunk=8192, unroll=1):
    nblocks = fc4.shape[1]
    repeat, collect, level = block_tables()

    def body(*refs):
        contract_body(chunk, unroll, *refs)

    return pl.pallas_call(
        body,
        out_shape=jax.ShapeDtypeStruct((NDEV, 4, COLS), F32),
        scratch_shapes=[
            pltpu.VMEM((2 * COLS, 2 * LANES), BF16),
            pltpu.VMEM((4 * COLS, 2 * LANES), F32),
        ],
        compiler_params=params(),
    )(
        received,
        jnp.asarray(repeat, BF16),
        jnp.asarray(collect, BF16),
        jnp.asarray(level),
        block_in.reshape(1, nblocks),
        block_out.reshape(1, nblocks),
        fc4,
    )


def targets_body(received, shell, target, out):
    rows = []
    for low in range(4):
        piece = received[:, low, :]
        rows.append(piece[0:32] + piece[32:64] + piece[64:96] + piece[96:128])
    renorm = jnp.concatenate(rows, 0)
    source = lax.broadcasted_iota(jnp.int32, (LANES, LANES), 0)
    order = lax.broadcasted_iota(jnp.int32, (LANES, LANES), 1)
    order = jnp.where(source == (order % 32) * 4 + order // 32, 1.0, 0.0)
    pad = jnp.zeros((5, LANES), F32)
    vectors = jnp.concatenate([shell[...].astype(F32), pad], 0)
    points = jnp.concatenate([target[...].astype(F32), pad], 0)
    vectors = jnp.dot(vectors, order, preferred_element_type=F32)
    index = lax.dot_general(
        points, vectors, (((0,), (0,)), ((), ())), preferred_element_type=F32
    )
    out[:, 0, :] = jnp.dot(
        sixteenth_cos(index), renorm, precision=HIGHEST, preferred_element_type=F32
    )
    out[:, 1, :] = jnp.dot(
        sixteenth_cos(index + 4.0), renorm, precision=HIGHEST, preferred_element_type=F32
    )


def to_targets(received, shell, target):
    return pl.pallas_call(
        targets_body,
        out_shape=jax.ShapeDtypeStruct((NDEV, 2, COLS), F32),
        compiler_params=params(),
    )(received, shell, target)


def arrange_body(received, out, turned):
    for comp in range(2):
        piece = received[:, comp, :]
        piece = jnp.concatenate([piece, jnp.zeros((NDEV, LANES - COLS), F32)], 1)
        turned[...] = piece.T
        for high in range(NPH):
            for alpha in range(3):
                out[0, 3 * alpha : 3 * alpha + 3, comp, LANES * high : LANES * high + LANES] = turned[
                    pl.ds(3 * high + alpha, 3, stride=24), :
                ]


def arrange(received):
    return pl.pallas_call(
        arrange_body,
        out_shape=jax.ShapeDtypeStruct((1, 9, 2, NPH * NDEV), F32),
        scratch_shapes=[pltpu.VMEM((LANES, LANES), F32)],
        compiler_params=params(),
    )(received)


def exchange(values):
    return lax.all_to_all(values, ALL, 0, 0, tiled=True)


def shards(
    modes, occup, qprime_coord, shell_vec, target_coord, pair_atoms, block_in, block_out, fc4
):
    picked = exchange(pick(modes, occup, qprime_coord, pair_atoms))
    density = exchange(to_shells(picked, shell_vec))
    renorm = exchange(contract(density, block_in, block_out, fc4))
    delta = exchange(to_targets(renorm, shell_vec, target_coord))
    return arrange(delta).transpose(0, 2, 1, 3)


def solution(mesh):
    return jax.shard_map(
        shards,
        mesh=mesh,
        in_specs=(
            P(("grp", "slab"), None, None, None),
            P(("grp", "slab"), None),
            P(None, ("grp", "slab")),
            P(),
            P(),
            P(),
            P(("grp", "slab")),
            P(("grp", "slab")),
            P(None, ("grp", "slab")),
        ),
        out_specs=P(("grp", "slab"), None, None, None),
        check_vma=False,
    )
```

```python
import math

import jax
import jax.numpy as jnp
import numpy as np
from jax import lax
from jax.experimental import pallas as pl
from jax.experimental.pallas import tpu as pltpu
from jax.sharding import PartitionSpec as P

MESH = 16
LANES = 128
NDEV = 128
NPH = 8
COLS = 72
MSG = 75
ALL = ("grp", "slab")
F32 = jnp.float32
BF16 = jnp.bfloat16
HIGHEST = lax.Precision.HIGHEST


def params(mebibytes=40):
    return pltpu.CompilerParams(vmem_limit_bytes=mebibytes * 1024 * 1024)


def sixteenth_cos(index):
    wrapped = index - 16.0 * jnp.floor(index * (1.0 / 16.0))
    folded = 4.0 - jnp.minimum(wrapped, 16.0 - wrapped)
    square = folded * folded
    poly = POLY[3]
    for coefficient in (POLY[2], POLY[1], POLY[0]):
        poly = poly * square + coefficient
    return folded * poly


def odd_polynomial():
    points = np.arange(1, 5, dtype=np.float64)
    values = np.sin(np.pi * points / 8.0)
    powers = np.stack([points ** (2 * k + 1) for k in range(4)], 1)
    return [float(c) for c in np.linalg.solve(powers, values)]


POLY = odd_polynomial()


def pick_body(
    coord, atoms, modes, occup, out, held, weights, pairs, spots, points, scaled, rows, dens, sems
):
    copies = [
        pltpu.make_async_copy(occup, weights, sems.at[4]),
        pltpu.make_async_copy(atoms, pairs, sems.at[5]),
        pltpu.make_async_copy(coord, points, sems.at[6]),
    ]
    loads = [pltpu.make_async_copy(modes.at[q], held.at[q], sems.at[q]) for q in range(4)]
    loads[0].start()
    for copy in copies:
        copy.start()
    for load in loads[1:]:
        load.start()
    copies[1].wait()
    first = pairs[0:1, :]
    second = pairs[1:2, :]
    turn = (128 - 3 * (first & 31)) & 127
    pairs[0:1, :] = ((first >> 5) * 3072 + second * 24) * 128 + turn
    move = pltpu.make_async_copy(pairs.at[0], spots, sems.at[7])
    move.start()
    copies[0].wait()
    for q in range(4):
        loads[q].wait()
        weight = weights[q : q + 1, :]
        for part in range(2):
            values = held[q, part]
            span = pl.ds(384 * part, 384)
            scaled[:, span] = (values.astype(F32) * weight).astype(BF16)
            for block in range(4):
                piece = values[96 * block : 96 * block + 96]
                rows[128 * block : 128 * block + 96, span] = piece
                other = piece if part == 1 else -piece
                low = 512 + 128 * block
                rows[low : low + 96, pl.ds(384 * (1 - part), 384)] = other
        for comp in range(2):
            for half in range(2):
                start = 512 * comp + 256 * half
                tile = lax.dot_general(
                    scaled[...],
                    rows[start : start + 256],
                    (((1,), (1,)), ((), ())),
                    preferred_element_type=F32,
                )
                for low in range(2):
                    base = 3072 * (2 * half + low) + 2 * q + comp
                    dens[pl.ds(base, 384, stride=8), :] = tile[:, 128 * low : 128 * low + 128]

    lane = lax.broadcasted_iota(jnp.int32, (8, LANES), 1)
    row = lax.broadcasted_iota(jnp.int32, (8, LANES), 0)
    copies[2].wait()
    move.wait()
    start = jnp.zeros((8, LANES), F32)
    for q in range(4):
        for axis in range(3):
            here = (row // 2 == q) & (lane == COLS + axis)
            start = jnp.where(here, points[axis, q].astype(F32), start)

    def one(dev, carry):
        acc = start
        for high in range(NPH):
            spot = spots[high * LANES + dev]
            base = spot >> 7
            for beta in range(3):
                low = 24 * beta + 3 * high
                value = dens[pl.ds(pl.multiple_of(base + 8 * beta, 8), 8), :]
                turned = pltpu.roll(value, (spot + low) & 127, 1)
                acc = jnp.where((lane >= low) & (lane < low + 3), turned, acc)
        out[dev] = acc[:, :MSG]
        return carry

    lax.fori_loop(0, NDEV, one, 0, unroll=16)


def pick(modes, occup, coord, atoms):
    anywhere = pl.BlockSpec(memory_space=pltpu.HBM)
    return pl.pallas_call(
        pick_body,
        in_specs=[anywhere] * 4,
        out_specs=pl.BlockSpec(memory_space=pltpu.VMEM),
        out_shape=jax.ShapeDtypeStruct((NDEV, 8, MSG), F32),
        scratch_shapes=[
            pltpu.VMEM((4, 2, 384, 384), BF16),
            pltpu.VMEM((4, 384), F32),
            pltpu.VMEM((2, NPH * LANES), jnp.int32),
            pltpu.SMEM((NPH * LANES,), jnp.int32),
            pltpu.SMEM((3, 4), jnp.int32),
            pltpu.VMEM((384, 768), BF16),
            pltpu.VMEM((1024, 768), BF16),
            pltpu.VMEM((4 * 384 * 8, LANES), F32),
            pltpu.SemaphoreType.DMA((8,)),
        ],
        compiler_params=params(60),
    )(coord, atoms, modes, occup)


def shells_body(received, shell, out):
    values = received[...].reshape(NDEV * 8, MSG)
    vectors = jnp.concatenate([jnp.zeros((COLS, LANES), F32), shell[...].astype(F32)], 0)
    index = lax.dot_general(
        vectors, values, (((0,), (1,)), ((), ())), preferred_element_type=F32
    )
    lane = lax.broadcasted_iota(jnp.int32, index.shape, 1)
    index = index + jnp.where(lane % 2 == 1, 4.0, 0.0)
    rho = jnp.dot(sixteenth_cos(index), values, precision=HIGHEST, preferred_element_type=F32)
    rho = rho[:, :COLS] * (1.0 / math.sqrt(512.0))
    for slab in range(32):
        piece = rho[4 * slab : 4 * slab + 4]
        for group in range(4):
            out[32 * group + slab] = piece


def to_shells(received, shell):
    return pl.pallas_call(
        shells_body,
        out_shape=jax.ShapeDtypeStruct((NDEV, 4, COLS), F32),
        compiler_params=params(),
    )(received, shell)


def block_tables():
    column = np.arange(2 * COLS)
    rest = column % COLS
    comp = 3 * (rest // 24) + rest % 3
    level = 8 * (column // COLS) + (rest % 24) // 3
    row = np.where(comp < 8, 8 * level + comp, 128 + level)
    place = (np.arange(2 * COLS)[:, None] == row[None, :]).astype(np.float32)
    first, second = np.arange(81) // 9, np.arange(81) % 9
    second = 3 * (second % 3) + second // 3
    row = np.where(first < 8, 8 * second + first, 72 + second)
    order = (np.arange(88)[:, None] == row[None, :]).astype(np.float32)
    return place, order


def two_parts(values):
    coarse = values.astype(BF16).astype(F32)
    return coarse, values - coarse


def contract_body(
    chunk, unroll, received, place, order, reads, writes, fc4, out, table, total
):
    for high in range(2):
        pieces = [received[:, 2 * high + low, :] for low in range(2)]
        parts = jnp.concatenate(two_parts(jnp.concatenate(pieces, 1)), 0).astype(BF16)
        turned = lax.dot_general(
            place[...].astype(BF16),
            parts,
            (((1,), (1,)), ((), ())),
            preferred_element_type=F32,
        ).astype(BF16)
        span = pl.ds(high * LANES, LANES)
        table[0:144, span] = turned[:, :LANES]
        table[144:288, span] = turned[:, LANES:]
    total[...] = jnp.zeros_like(total)
    level = lax.broadcasted_iota(jnp.int32, (16, chunk), 0)
    level_pair = (level >> 3).astype(BF16)
    level_all = level.astype(BF16)
    low_place = lax.broadcasted_iota(jnp.int32, (2 * LANES, chunk), 0).astype(BF16)
    unit, zero = jnp.ones((), BF16), jnp.zeros((), BF16)

    def small(values):
        return values.astype(F32).astype(BF16)

    def low_hot(entry):
        low = ((entry >> 11) << 7) | (entry & 127)
        return jnp.where(low_place == small(low), unit, zero)

    def one(step, carry):
        span = pl.ds(pl.multiple_of(step * chunk, chunk), chunk)
        coeff = jnp.dot(order[...], fc4[:, span], preferred_element_type=F32)
        read, write = reads[:, span], writes[:, span]
        read_high = (read >> 7) & 15
        write_high = small((write >> 7) & 15)
        found = jnp.dot(table[...], low_hot(read), preferred_element_type=F32)
        found = found[:144] + found[144:]
        main = found[0:8]
        for high in range(1, 16):
            main = jnp.where(read_high == high, found[8 * high : 8 * high + 8], main)
        last = jnp.sum(jnp.where(level == read_high, found[128:144], 0.0), 0, keepdims=True)
        contrib = coeff[64:72] * last
        for comp in range(8):
            contrib = contrib + coeff[8 * comp : 8 * comp + 8] * main[comp : comp + 1]
        ninth = jnp.sum(coeff[72:80] * main, 0, keepdims=True) + coeff[80:81] * last
        spread = []
        for body, tail in zip(two_parts(contrib), two_parts(ninth)):
            body = jnp.concatenate([body, body], 0).astype(BF16)
            tail = jnp.broadcast_to(tail, level.shape).astype(BF16)
            for pair in range(8):
                spread.append(jnp.where(level_pair + 2 * pair == write_high, body, zero))
            spread.append(jnp.where(level_all == write_high, tail, zero))
        total[...] += lax.dot_general(
            jnp.concatenate(spread, 0),
            low_hot(write),
            (((1,), (1,)), ((), ())),
            preferred_element_type=F32,
        )
        return carry

    lax.fori_loop(0, fc4.shape[1] // chunk, one, 0, unroll=unroll)
    for shell in range(4):
        low, span = shell % 2, pl.ds(shell // 2 * LANES, LANES)
        body = total[64 * low : 64 * low + 64, span] + total[144 + 64 * low : 208 + 64 * low, span]
        tail = total[128 + 8 * low : 136 + 8 * low, span] + total[272 + 8 * low : 280 + 8 * low, span]
        rest = jnp.zeros((LANES - COLS, LANES), F32)
        out[:, shell, :] = jnp.concatenate([body, tail, rest], 0).T[:, :COLS]


def contract(received, block_in, block_out, fc4, chunk=16384, unroll=1):
    nblocks = fc4.shape[1]
    place, order = block_tables()
    reads, writes = block_in.reshape(1, nblocks), block_out.reshape(1, nblocks)

    def body(*refs):
        contract_body(chunk, unroll, *refs)

    return pl.pallas_call(
        body,
        out_shape=jax.ShapeDtypeStruct((NDEV, 4, COLS), F32),
        scratch_shapes=[
            pltpu.VMEM((4 * COLS, 2 * LANES), BF16),
            pltpu.VMEM((4 * COLS, 2 * LANES), F32),
        ],
        compiler_params=params(),
    )(received, jnp.asarray(place), jnp.asarray(order, BF16), reads, writes, fc4)


def targets_body(received, shell, target, out):
    rows = []
    for low in range(4):
        piece = received[:, low, :]
        rows.append(piece[0:32] + piece[32:64] + piece[64:96] + piece[96:128])
    renorm = jnp.concatenate(rows, 0)
    source = lax.broadcasted_iota(jnp.int32, (LANES, LANES), 0)
    order = lax.broadcasted_iota(jnp.int32, (LANES, LANES), 1)
    order = jnp.where(source == (order % 32) * 4 + order // 32, 1.0, 0.0)
    pad = jnp.zeros((5, LANES), F32)
    vectors = jnp.concatenate([shell[...].astype(F32), pad], 0)
    points = jnp.concatenate([target[...].astype(F32), pad], 0)
    vectors = jnp.dot(vectors, order, preferred_element_type=F32)
    index = lax.dot_general(
        points, vectors, (((0,), (0,)), ((), ())), preferred_element_type=F32
    )
    out[:, 0, :] = jnp.dot(
        sixteenth_cos(index), renorm, precision=HIGHEST, preferred_element_type=F32
    )
    out[:, 1, :] = jnp.dot(
        sixteenth_cos(index + 4.0), renorm, precision=HIGHEST, preferred_element_type=F32
    )


def to_targets(received, shell, target):
    return pl.pallas_call(
        targets_body,
        out_shape=jax.ShapeDtypeStruct((NDEV, 2, COLS), F32),
        compiler_params=params(),
    )(received, shell, target)


def arrange_body(received, out):
    for comp in range(2):
        piece = received[:, comp, :]
        piece = jnp.concatenate([piece, jnp.zeros((NDEV, LANES - COLS), F32)], 1).T
        for high in range(NPH):
            span = pl.ds(LANES * high, LANES)
            out[0, 0:8, comp, span] = piece[8 * high : 8 * high + 8]
            out[0, 8:9, comp, span] = piece[64 + high : 65 + high]


def arrange(received):
    return pl.pallas_call(
        arrange_body,
        out_shape=jax.ShapeDtypeStruct((1, 9, 2, NPH * NDEV), F32),
        compiler_params=params(),
    )(received)


def exchange(values):
    return lax.all_to_all(values, ALL, 0, 0, tiled=True)


def shards(
    modes, occup, qprime_coord, shell_vec, target_coord, pair_atoms, block_in, block_out, fc4
):
    picked = exchange(pick(modes, occup, qprime_coord, pair_atoms))
    density = exchange(to_shells(picked, shell_vec))
    renorm = exchange(contract(density, block_in, block_out, fc4))
    delta = exchange(to_targets(renorm, shell_vec, target_coord))
    return arrange(delta).transpose(0, 2, 1, 3)


def solution(mesh):
    return jax.shard_map(
        shards,
        mesh=mesh,
        in_specs=(
            P(("grp", "slab"), None, None, None),
            P(("grp", "slab"), None),
            P(None, ("grp", "slab")),
            P(),
            P(),
            P(),
            P(("grp", "slab")),
            P(("grp", "slab")),
            P(None, ("grp", "slab")),
        ),
        out_specs=P(("grp", "slab"), None, None, None),
        check_vma=False,
    )
```

```python
import math

import jax
import jax.numpy as jnp
import numpy as np
from jax import lax
from jax.experimental import pallas as pl
from jax.experimental.pallas import tpu as pltpu
from jax.sharding import PartitionSpec as P

MESH = 16
LANES = 128
NDEV = 128
NPH = 8
COLS = 72
PITCH = 4 * 384 + 8
MSG = 75
ALL = ("grp", "slab")
F32 = jnp.float32
BF16 = jnp.bfloat16
HIGHEST = lax.Precision.HIGHEST


def params(mebibytes=40):
    return pltpu.CompilerParams(vmem_limit_bytes=mebibytes * 1024 * 1024)


def sixteenth_cos(index):
    wrapped = index - 16.0 * jnp.floor(index * (1.0 / 16.0))
    folded = 4.0 - jnp.minimum(wrapped, 16.0 - wrapped)
    square = folded * folded
    poly = POLY[3]
    for coefficient in (POLY[2], POLY[1], POLY[0]):
        poly = poly * square + coefficient
    return folded * poly


def odd_polynomial():
    points = np.arange(1, 5, dtype=np.float64)
    values = np.sin(np.pi * points / 8.0)
    powers = np.stack([points ** (2 * k + 1) for k in range(4)], 1)
    return [float(c) for c in np.linalg.solve(powers, values)]


POLY = odd_polynomial()


def pick_body(
    coord, atoms, modes, occup, out, held, weights, pairs, spots, points, scaled, rows, dens, sems
):
    copies = [
        pltpu.make_async_copy(occup, weights, sems.at[4]),
        pltpu.make_async_copy(atoms, pairs, sems.at[5]),
        pltpu.make_async_copy(coord, points, sems.at[6]),
    ]
    loads = [pltpu.make_async_copy(modes.at[q], held.at[q], sems.at[q]) for q in range(4)]
    loads[0].start()
    for copy in copies:
        copy.start()
    for load in loads[1:]:
        load.start()
    copies[1].wait()
    first = pairs[0:1, :]
    second = pairs[1:2, :]
    turn = (128 - 3 * (second & 31)) & 127
    pairs[0:1, :] = ((second >> 5) * 384 + first * 3) * 128 + turn
    move = pltpu.make_async_copy(pairs.at[0], spots, sems.at[7])
    move.start()
    copies[0].wait()
    for q in range(4):
        loads[q].wait()
        weight = weights[q : q + 1, :]
        real, imag = held[q, 0], held[q, 1]
        rows[q % 2, 0:384, 0:384] = real
        rows[q % 2, 0:384, 384:768] = imag
        rows[q % 2, 384:768, 0:384] = imag
        rows[q % 2, 384:768, 384:768] = -real
        for part in range(2):
            values = (held[q, part].astype(F32) * weight).astype(BF16)
            for block in range(4):
                scaled[q % 2, 128 * block : 128 * block + 96, pl.ds(384 * part, 384)] = values[
                    96 * block : 96 * block + 96
                ]
        for comp in range(2):
            for half in range(2):
                tile = lax.dot_general(
                    rows[q % 2, 384 * comp : 384 * comp + 384],
                    scaled[q % 2, 256 * half : 256 * half + 256],
                    (((1,), (1,)), ((), ())),
                    preferred_element_type=F32,
                )
                for low in range(2):
                    base = PITCH * (2 * q + comp) + 384 * (2 * half + low)
                    dens[pl.ds(base, 384), :] = tile[:, 128 * low : 128 * low + 128]

    lane = lax.broadcasted_iota(jnp.int32, (8, LANES), 1)
    row = lax.broadcasted_iota(jnp.int32, (8, LANES), 0)
    copies[2].wait()
    move.wait()
    start = jnp.zeros((8, LANES), F32)
    for q in range(4):
        for axis in range(3):
            here = (row // 2 == q) & (lane == COLS + axis)
            start = jnp.where(here, points[axis, q].astype(F32), start)

    def one(dev, carry):
        acc = start
        for high in range(NPH):
            spot = spots[high * LANES + dev]
            base = spot >> 7
            for alpha in range(3):
                low = 24 * alpha + 3 * high
                value = dens[pl.ds(base + alpha, 8, stride=PITCH), :]
                turned = pltpu.roll(value, (spot + low) & 127, 1)
                acc = jnp.where((lane >= low) & (lane < low + 3), turned, acc)
        out[dev] = acc[:, :MSG]
        return carry

    lax.fori_loop(0, NDEV, one, 0, unroll=64)


def pick(modes, occup, coord, atoms):
    anywhere = pl.BlockSpec(memory_space=pltpu.HBM)
    return pl.pallas_call(
        pick_body,
        in_specs=[anywhere] * 4,
        out_specs=pl.BlockSpec(memory_space=pltpu.VMEM),
        out_shape=jax.ShapeDtypeStruct((NDEV, 8, MSG), F32),
        scratch_shapes=[
            pltpu.VMEM((4, 2, 384, 384), BF16),
            pltpu.VMEM((4, 384), F32),
            pltpu.VMEM((2, NPH * LANES), jnp.int32),
            pltpu.SMEM((NPH * LANES,), jnp.int32),
            pltpu.SMEM((3, 4), jnp.int32),
            pltpu.VMEM((2, 512, 768), BF16),
            pltpu.VMEM((2, 768, 768), BF16),
            pltpu.VMEM((PITCH * 8, LANES), F32),
            pltpu.SemaphoreType.DMA((8,)),
        ],
        compiler_params=params(60),
    )(coord, atoms, modes, occup)


def shells_body(received, shell, out):
    values = received[...].reshape(NDEV * 8, MSG)
    vectors = jnp.concatenate([jnp.zeros((COLS, LANES), F32), shell[...].astype(F32)], 0)
    index = lax.dot_general(
        vectors, values, (((0,), (1,)), ((), ())), preferred_element_type=F32
    )
    lane = lax.broadcasted_iota(jnp.int32, index.shape, 1)
    index = index + jnp.where(lane % 2 == 1, 4.0, 0.0)
    rho = jnp.dot(sixteenth_cos(index), values, precision=HIGHEST, preferred_element_type=F32)
    rho = rho[:, :COLS] * (1.0 / math.sqrt(512.0))
    for slab in range(32):
        piece = rho[4 * slab : 4 * slab + 4]
        for group in range(4):
            out[32 * group + slab] = piece


def to_shells(received, shell):
    return pl.pallas_call(
        shells_body,
        out_shape=jax.ShapeDtypeStruct((NDEV, 4, COLS), F32),
        compiler_params=params(),
    )(received, shell)


def block_tables():
    column = np.arange(2 * COLS)
    rest = column % COLS
    comp = 3 * (rest // 24) + rest % 3
    level = 8 * (column // COLS) + (rest % 24) // 3
    row = np.where(comp < 8, 8 * level + comp, 128 + level)
    place = (np.arange(2 * COLS)[:, None] == row[None, :]).astype(np.float32)
    first, second = np.arange(81) // 9, np.arange(81) % 9
    row = np.where(first < 8, 8 * second + first, 72 + second)
    order = (np.arange(88)[:, None] == row[None, :]).astype(np.float32)
    return place, order


def two_parts(values):
    coarse = values.astype(BF16).astype(F32)
    return coarse, values - coarse


def contract_body(
    chunk, unroll, received, place, order, reads, writes, fc4, out, table, total
):
    for high in range(2):
        pieces = [received[:, 2 * high + low, :] for low in range(2)]
        parts = jnp.concatenate(two_parts(jnp.concatenate(pieces, 1)), 0).astype(BF16)
        turned = lax.dot_general(
            place[...].astype(BF16),
            parts,
            (((1,), (1,)), ((), ())),
            preferred_element_type=F32,
        ).astype(BF16)
        span = pl.ds(high * LANES, LANES)
        table[0:144, span] = turned[:, :LANES]
        table[144:288, span] = turned[:, LANES:]
    total[...] = jnp.zeros_like(total)
    level = lax.broadcasted_iota(jnp.int32, (16, chunk), 0)
    level_pair = (level >> 3).astype(BF16)
    level_all = level.astype(BF16)
    low_place = lax.broadcasted_iota(jnp.int32, (2 * LANES, chunk), 0).astype(BF16)
    unit, zero = jnp.ones((), BF16), jnp.zeros((), BF16)

    def small(values):
        return values.astype(F32).astype(BF16)

    def low_hot(entry):
        low = ((entry >> 11) << 7) | (entry & 127)
        return jnp.where(low_place == small(low), unit, zero)

    def one(step, carry):
        span = pl.ds(pl.multiple_of(step * chunk, chunk), chunk)
        coeff = jnp.dot(order[...], fc4[:, span], preferred_element_type=F32)
        read, write = reads[:, span], writes[:, span]
        read_high = (read >> 7) & 15
        write_high = small((write >> 7) & 15)
        found = jnp.dot(table[...], low_hot(read), preferred_element_type=F32)
        found = found[:144] + found[144:]
        main = found[0:8]
        for high in range(1, 16):
            main = jnp.where(read_high == high, found[8 * high : 8 * high + 8], main)
        last = jnp.sum(jnp.where(level == read_high, found[128:144], 0.0), 0, keepdims=True)
        contrib = coeff[64:72] * last
        for comp in range(8):
            contrib = contrib + coeff[8 * comp : 8 * comp + 8] * main[comp : comp + 1]
        ninth = jnp.sum(coeff[72:80] * main, 0, keepdims=True) + coeff[80:81] * last
        spread = []
        for body, tail in zip(two_parts(contrib), two_parts(ninth)):
            body = jnp.concatenate([body, body], 0).astype(BF16)
            tail = jnp.broadcast_to(tail, level.shape).astype(BF16)
            for pair in range(8):
                spread.append(jnp.where(level_pair + 2 * pair == write_high, body, zero))
            spread.append(jnp.where(level_all == write_high, tail, zero))
        total[...] += lax.dot_general(
            jnp.concatenate(spread, 0),
            low_hot(write),
            (((1,), (1,)), ((), ())),
            preferred_element_type=F32,
        )
        return carry

    lax.fori_loop(0, fc4.shape[1] // chunk, one, 0, unroll=unroll)
    for shell in range(4):
        low, span = shell % 2, pl.ds(shell // 2 * LANES, LANES)
        body = total[64 * low : 64 * low + 64, span] + total[144 + 64 * low : 208 + 64 * low, span]
        tail = total[128 + 8 * low : 136 + 8 * low, span] + total[272 + 8 * low : 280 + 8 * low, span]
        rest = jnp.zeros((LANES - COLS, LANES), F32)
        out[:, shell, :] = jnp.concatenate([body, tail, rest], 0).T[:, :COLS]


def contract(received, block_in, block_out, fc4, chunk=16384, unroll=1):
    nblocks = fc4.shape[1]
    place, order = block_tables()
    reads, writes = block_in.reshape(1, nblocks), block_out.reshape(1, nblocks)

    def body(*refs):
        contract_body(chunk, unroll, *refs)

    return pl.pallas_call(
        body,
        out_shape=jax.ShapeDtypeStruct((NDEV, 4, COLS), F32),
        scratch_shapes=[
            pltpu.VMEM((4 * COLS, 2 * LANES), BF16),
            pltpu.VMEM((4 * COLS, 2 * LANES), F32),
        ],
        compiler_params=params(),
    )(received, jnp.asarray(place), jnp.asarray(order, BF16), reads, writes, fc4)


def targets_body(received, shell, target, out):
    rows = []
    for low in range(4):
        piece = received[:, low, :]
        rows.append(piece[0:32] + piece[32:64] + piece[64:96] + piece[96:128])
    renorm = jnp.concatenate(rows, 0)
    source = lax.broadcasted_iota(jnp.int32, (LANES, LANES), 0)
    order = lax.broadcasted_iota(jnp.int32, (LANES, LANES), 1)
    order = jnp.where(source == (order % 32) * 4 + order // 32, 1.0, 0.0)
    pad = jnp.zeros((5, LANES), F32)
    vectors = jnp.concatenate([shell[...].astype(F32), pad], 0)
    points = jnp.concatenate([target[...].astype(F32), pad], 0)
    vectors = jnp.dot(vectors, order, preferred_element_type=F32)
    index = lax.dot_general(
        points, vectors, (((0,), (0,)), ((), ())), preferred_element_type=F32
    )
    out[:, 0, :] = jnp.dot(
        sixteenth_cos(index), renorm, precision=HIGHEST, preferred_element_type=F32
    )
    out[:, 1, :] = jnp.dot(
        sixteenth_cos(index + 4.0), renorm, precision=HIGHEST, preferred_element_type=F32
    )


def to_targets(received, shell, target):
    return pl.pallas_call(
        targets_body,
        out_shape=jax.ShapeDtypeStruct((NDEV, 2, COLS), F32),
        compiler_params=params(),
    )(received, shell, target)


def arrange_body(received, out):
    for comp in range(2):
        piece = received[:, comp, :]
        piece = jnp.concatenate([piece, jnp.zeros((NDEV, LANES - COLS), F32)], 1).T
        for high in range(NPH):
            span = pl.ds(LANES * high, LANES)
            out[0, 0:8, comp, span] = piece[8 * high : 8 * high + 8]
            out[0, 8:9, comp, span] = piece[64 + high : 65 + high]


def arrange(received):
    return pl.pallas_call(
        arrange_body,
        out_shape=jax.ShapeDtypeStruct((1, 9, 2, NPH * NDEV), F32),
        compiler_params=params(),
    )(received)


def exchange(values):
    return lax.all_to_all(values, ALL, 0, 0, tiled=True)


def shards(
    modes, occup, qprime_coord, shell_vec, target_coord, pair_atoms, block_in, block_out, fc4
):
    picked = exchange(pick(modes, occup, qprime_coord, pair_atoms))
    density = exchange(to_shells(picked, shell_vec))
    renorm = exchange(contract(density, block_in, block_out, fc4))
    delta = exchange(to_targets(renorm, shell_vec, target_coord))
    return arrange(delta).transpose(0, 2, 1, 3)


def solution(mesh):
    return jax.shard_map(
        shards,
        mesh=mesh,
        in_specs=(
            P(("grp", "slab"), None, None, None),
            P(("grp", "slab"), None),
            P(None, ("grp", "slab")),
            P(),
            P(),
            P(),
            P(("grp", "slab")),
            P(("grp", "slab")),
            P(None, ("grp", "slab")),
        ),
        out_specs=P(("grp", "slab"), None, None, None),
        check_vma=False,
    )
```

```python
import math

import jax
import jax.numpy as jnp
import numpy as np
from jax import lax
from jax.experimental import pallas as pl
from jax.experimental.pallas import tpu as pltpu
from jax.sharding import PartitionSpec as P

MESH = 16
LANES = 128
NDEV = 128
NPH = 8
COLS = 72
PITCH = 4 * 384 + 8
FIRST = 5
OTHER = 3
ALL = ("grp", "slab")
F32 = jnp.float32
BF16 = jnp.bfloat16
HIGHEST = lax.Precision.HIGHEST


def params(mebibytes=40):
    return pltpu.CompilerParams(vmem_limit_bytes=mebibytes * 1024 * 1024)


def sixteenth_cos(index):
    wrapped = index - 16.0 * jnp.floor(index * (1.0 / 16.0))
    folded = 4.0 - jnp.minimum(wrapped, 16.0 - wrapped)
    square = folded * folded
    poly = POLY[3]
    for coefficient in (POLY[2], POLY[1], POLY[0]):
        poly = poly * square + coefficient
    return folded * poly


def odd_polynomial():
    points = np.arange(1, 5, dtype=np.float64)
    values = np.sin(np.pi * points / 8.0)
    powers = np.stack([points ** (2 * k + 1) for k in range(4)], 1)
    return [float(c) for c in np.linalg.solve(powers, values)]


POLY = odd_polynomial()


def pick_body(
    coord, atoms, modes, occup, out, held, weights, pairs, spots, points, scaled, rows, dens, picked, sems
):
    copies = [
        pltpu.make_async_copy(occup, weights, sems.at[4]),
        pltpu.make_async_copy(atoms, pairs, sems.at[5]),
        pltpu.make_async_copy(coord, points, sems.at[6]),
    ]
    loads = [pltpu.make_async_copy(modes.at[q], held.at[q], sems.at[q]) for q in range(4)]
    loads[0].start()
    for copy in copies:
        copy.start()
    for load in loads[1:]:
        load.start()
    copies[1].wait()
    first = pairs[0:1, :]
    second = pairs[1:2, :]
    turn = (128 - 3 * (second & 31)) & 127
    pairs[0:1, :] = ((second >> 5) * 384 + first * 3) * 128 + turn
    move = pltpu.make_async_copy(pairs.at[0], spots, sems.at[7])
    move.start()
    copies[0].wait()
    for q in range(4):
        loads[q].wait()
        weight = weights[q : q + 1, :]
        real, imag = held[q, 0], held[q, 1]
        rows[q % 2, 0:384, 0:384] = real
        rows[q % 2, 0:384, 384:768] = imag
        rows[q % 2, 384:768, 0:384] = imag
        rows[q % 2, 384:768, 384:768] = -real
        for part in range(2):
            values = (held[q, part].astype(F32) * weight).astype(BF16)
            for block in range(4):
                scaled[q % 2, 128 * block : 128 * block + 96, pl.ds(384 * part, 384)] = values[
                    96 * block : 96 * block + 96
                ]
        for comp in range(2):
            for half in range(2):
                tile = lax.dot_general(
                    rows[q % 2, 384 * comp : 384 * comp + 384],
                    scaled[q % 2, 256 * half : 256 * half + 256],
                    (((1,), (1,)), ((), ())),
                    preferred_element_type=F32,
                )
                for low in range(2):
                    base = PITCH * (2 * q + comp) + 384 * (2 * half + low)
                    dens[pl.ds(base, 384), :] = tile[:, 128 * low : 128 * low + 128]

    lane = lax.broadcasted_iota(jnp.int32, (8, LANES), 1)
    copies[2].wait()
    move.wait()

    def one(dev, carry):
        acc = jnp.zeros((8, LANES), F32)
        for high in range(NPH):
            spot = spots[high * LANES + dev]
            base = spot >> 7
            for alpha in range(3):
                low = 24 * alpha + 3 * high
                value = dens[pl.ds(base + alpha, 8, stride=PITCH), :]
                turned = pltpu.roll(value, (spot + low) & 127, 1)
                acc = jnp.where((lane >= low) & (lane < low + 3), turned, acc)
        picked[pl.ds(pl.multiple_of(8 * dev, 8), 8), :] = acc
        return carry

    lax.fori_loop(0, NDEV, one, 0, unroll=64)
    lane = lax.broadcasted_iota(jnp.int32, (NDEV, LANES), 1)
    parts = [picked[pl.ds(part, NDEV, stride=8), :] for part in range(8)]
    for part in range(4):
        joined = jnp.where(lane < 64, parts[part], pltpu.roll(parts[part + 4], 64, 1))
        out[pl.ds(part, NDEV, stride=FIRST), :] = joined
    column = lax.broadcasted_iota(jnp.int32, (1, LANES), 1)
    last = jnp.zeros((1, LANES), F32)
    for q in range(4):
        for axis in range(3):
            last = jnp.where(column == 64 + 8 * q + axis, points[axis, q].astype(F32), last)
    last = jnp.broadcast_to(last, (NDEV, LANES))
    for part in range(8):
        piece = pltpu.roll(parts[part], (8 * part + 64) % LANES, 1)
        last = jnp.where((lane >= 8 * part) & (lane < 8 * part + 8), piece, last)
    out[pl.ds(4, NDEV, stride=FIRST), :] = last


def pick(modes, occup, coord, atoms):
    anywhere = pl.BlockSpec(memory_space=pltpu.HBM)
    return pl.pallas_call(
        pick_body,
        in_specs=[anywhere] * 4,
        out_specs=pl.BlockSpec(memory_space=pltpu.VMEM),
        out_shape=jax.ShapeDtypeStruct((NDEV * FIRST, LANES), F32),
        scratch_shapes=[
            pltpu.VMEM((4, 2, 384, 384), BF16),
            pltpu.VMEM((4, 384), F32),
            pltpu.VMEM((2, NPH * LANES), jnp.int32),
            pltpu.SMEM((NPH * LANES,), jnp.int32),
            pltpu.SMEM((3, 4), jnp.int32),
            pltpu.VMEM((2, 512, 768), BF16),
            pltpu.VMEM((2, 768, 768), BF16),
            pltpu.VMEM((PITCH * 8, LANES), F32),
            pltpu.VMEM((8 * NDEV, LANES), F32),
            pltpu.SemaphoreType.DMA((8,)),
        ],
        compiler_params=params(60),
    )(coord, atoms, modes, occup)


def two_parts(values):
    coarse = values.astype(BF16).astype(F32)
    return coarse, values - coarse


def split_dot(left, right):
    left_high, left_low = [part.astype(BF16) for part in two_parts(left)]
    right_high, right_low = [part.astype(BF16) for part in two_parts(right)]
    total = jnp.dot(left_high, right_high, preferred_element_type=F32)
    total = total + jnp.dot(left_high, right_low, preferred_element_type=F32)
    return total + jnp.dot(left_low, right_high, preferred_element_type=F32)


def pack(shells):
    lane = lax.broadcasted_iota(jnp.int32, shells[0].shape, 1)
    return [
        jnp.where(lane < COLS, shells[j], pltpu.roll(shells[3], COLS - 24 * j, 1)) for j in range(3)
    ]


def unpack(rows):
    lane = lax.broadcasted_iota(jnp.int32, rows[0].shape, 1)
    turned = [pltpu.roll(rows[j], LANES - COLS + 24 * j, 1) for j in range(3)]
    last = jnp.where(lane < 24, turned[0], jnp.where(lane < 48, turned[1], turned[2]))
    return [*rows, last]


def shells_body(received, shell, out, summed):
    parts = [received[pl.ds(part, NDEV, stride=FIRST), :] for part in range(FIRST)]
    vector = jnp.concatenate([shell[...].astype(F32), jnp.zeros((5, LANES), F32)], 0)
    vectors = [
        jnp.concatenate(
            [jnp.zeros((64 + 8 * q, LANES), F32), vector, jnp.zeros((56 - 8 * q, LANES), F32)], 0
        )
        for q in range(4)
    ]
    index = lax.dot_general(
        jnp.concatenate(vectors, 1),
        parts[4],
        (((0,), (1,)), ((), ())),
        preferred_element_type=F32,
    )
    waves = [sixteenth_cos(index), sixteenth_cos(index + 4.0)]
    waves = [waves[part % 2][LANES * (part // 2) : LANES * (part // 2 + 1)] for part in range(8)]
    values = jnp.concatenate(parts[:4], 0)
    first = split_dot(jnp.concatenate(waves[:4], 1), values)
    second = split_dot(jnp.concatenate(waves[4:], 1), values)
    rest = [pltpu.roll(parts[4], (LANES - 8 * part) % LANES, 1) for part in range(8)]
    rest = split_dot(jnp.concatenate(waves, 1), jnp.concatenate(rest, 0))
    lane = lax.broadcasted_iota(jnp.int32, (LANES, LANES), 1)
    rho = jnp.where(lane < 64, first + pltpu.roll(second, 64, 1), pltpu.roll(rest, 64, 1))
    summed[...] = rho * (1.0 / math.sqrt(512.0))
    rows = pack([summed[pl.ds(low, 32, stride=4), :] for low in range(4)])
    for j in range(3):
        for group in range(4):
            out[pl.ds(OTHER * 32 * group + j, 32, stride=OTHER), :] = rows[j]


def to_shells(received, shell):
    return pl.pallas_call(
        shells_body,
        out_shape=jax.ShapeDtypeStruct((NDEV * OTHER, LANES), F32),
        scratch_shapes=[pltpu.VMEM((LANES, LANES), F32)],
        compiler_params=params(),
    )(received, shell)


def block_tables():
    column = np.arange(2 * COLS)
    rest = column % COLS
    comp = 3 * (rest // 24) + rest % 3
    level = 8 * (column // COLS) + (rest % 24) // 3
    row = np.where(comp < 8, 8 * level + comp, 128 + level)
    place = (np.arange(2 * COLS)[:, None] == row[None, :]).astype(np.float32)
    first, second = np.arange(81) // 9, np.arange(81) % 9
    row = np.where(first < 8, 8 * second + first, 72 + second)
    order = (np.arange(88)[:, None] == row[None, :]).astype(np.float32)
    return place, order


def contract_body(
    chunk, unroll, received, place, order, reads, writes, fc4, out, table, total
):
    shells = unpack([received[pl.ds(j, NDEV, stride=OTHER), :] for j in range(3)])
    for high in range(2):
        pieces = [shells[2 * high + low][:, :COLS] for low in range(2)]
        parts = jnp.concatenate(two_parts(jnp.concatenate(pieces, 1)), 0).astype(BF16)
        turned = lax.dot_general(
            place[...].astype(BF16),
            parts,
            (((1,), (1,)), ((), ())),
            preferred_element_type=F32,
        ).astype(BF16)
        span = pl.ds(high * LANES, LANES)
        table[0:144, span] = turned[:, :LANES]
        table[144:288, span] = turned[:, LANES:]
    total[...] = jnp.zeros_like(total)
    level = lax.broadcasted_iota(jnp.int32, (16, chunk), 0)
    level_pair = (level >> 3).astype(BF16)
    level_all = level.astype(BF16)
    low_place = lax.broadcasted_iota(jnp.int32, (2 * LANES, chunk), 0).astype(BF16)
    unit, zero = jnp.ones((), BF16), jnp.zeros((), BF16)

    def small(values):
        return values.astype(F32).astype(BF16)

    def low_hot(entry):
        low = ((entry >> 11) << 7) | (entry & 127)
        return jnp.where(low_place == small(low), unit, zero)

    def one(step, carry):
        span = pl.ds(pl.multiple_of(step * chunk, chunk), chunk)
        coeff = jnp.dot(order[...], fc4[:, span], preferred_element_type=F32)
        read, write = reads[:, span], writes[:, span]
        read_high = (read >> 7) & 15
        write_high = small((write >> 7) & 15)
        found = jnp.dot(table[...], low_hot(read), preferred_element_type=F32)
        found = found[:144] + found[144:]
        main = found[0:8]
        for high in range(1, 16):
            main = jnp.where(read_high == high, found[8 * high : 8 * high + 8], main)
        last = jnp.sum(jnp.where(level == read_high, found[128:144], 0.0), 0, keepdims=True)
        contrib = coeff[64:72] * last
        for comp in range(8):
            contrib = contrib + coeff[8 * comp : 8 * comp + 8] * main[comp : comp + 1]
        ninth = jnp.sum(coeff[72:80] * main, 0, keepdims=True) + coeff[80:81] * last
        spread = []
        for body, tail in zip(two_parts(contrib), two_parts(ninth)):
            body = jnp.concatenate([body, body], 0).astype(BF16)
            tail = jnp.broadcast_to(tail, level.shape).astype(BF16)
            for pair in range(8):
                spread.append(jnp.where(level_pair + 2 * pair == write_high, body, zero))
            spread.append(jnp.where(level_all == write_high, tail, zero))
        total[...] += lax.dot_general(
            jnp.concatenate(spread, 0),
            low_hot(write),
            (((1,), (1,)), ((), ())),
            preferred_element_type=F32,
        )
        return carry

    lax.fori_loop(0, fc4.shape[1] // chunk, one, 0, unroll=unroll)
    shells = []
    for shell in range(4):
        low, span = shell % 2, pl.ds(shell // 2 * LANES, LANES)
        body = total[64 * low : 64 * low + 64, span] + total[144 + 64 * low : 208 + 64 * low, span]
        tail = total[128 + 8 * low : 136 + 8 * low, span] + total[272 + 8 * low : 280 + 8 * low, span]
        rest = jnp.zeros((LANES - COLS, LANES), F32)
        shells.append(jnp.concatenate([body, tail, rest], 0).T)
    for j, row in enumerate(pack(shells)):
        out[pl.ds(j, NDEV, stride=OTHER), :] = row


def contract(received, block_in, block_out, fc4, chunk=16384, unroll=1):
    nblocks = fc4.shape[1]
    place, order = block_tables()
    reads, writes = block_in.reshape(1, nblocks), block_out.reshape(1, nblocks)

    def body(*refs):
        contract_body(chunk, unroll, *refs)

    return pl.pallas_call(
        body,
        out_shape=jax.ShapeDtypeStruct((NDEV * OTHER, LANES), F32),
        scratch_shapes=[
            pltpu.VMEM((4 * COLS, 2 * LANES), BF16),
            pltpu.VMEM((4 * COLS, 2 * LANES), F32),
        ],
        compiler_params=params(),
    )(received, jnp.asarray(place), jnp.asarray(order, BF16), reads, writes, fc4)


def targets_body(received, shell, target, out):
    rows = []
    for j in range(3):
        piece = received[pl.ds(j, NDEV, stride=OTHER), :]
        rows.append(piece[0:32] + piece[32:64] + piece[64:96] + piece[96:128])
    renorm = jnp.concatenate(unpack(rows), 0)
    source = lax.broadcasted_iota(jnp.int32, (LANES, LANES), 0)
    order = lax.broadcasted_iota(jnp.int32, (LANES, LANES), 1)
    order = jnp.where(source == (order % 32) * 4 + order // 32, 1.0, 0.0)
    pad = jnp.zeros((5, LANES), F32)
    vectors = jnp.concatenate([shell[...].astype(F32), pad], 0)
    points = jnp.concatenate([target[...].astype(F32), pad], 0)
    vectors = jnp.dot(vectors, order, preferred_element_type=F32)
    index = lax.dot_general(
        points, vectors, (((0,), (0,)), ((), ())), preferred_element_type=F32
    )
    out[:, 0, :] = split_dot(sixteenth_cos(index), renorm)[:, :COLS]
    out[:, 1, :] = split_dot(sixteenth_cos(index + 4.0), renorm)[:, :COLS]


def to_targets(received, shell, target):
    return pl.pallas_call(
        targets_body,
        out_shape=jax.ShapeDtypeStruct((NDEV, 2, COLS), F32),
        compiler_params=params(),
    )(received, shell, target)


def arrange_body(received, out):
    for comp in range(2):
        piece = received[:, comp, :]
        piece = jnp.concatenate([piece, jnp.zeros((NDEV, LANES - COLS), F32)], 1).T
        for high in range(NPH):
            span = pl.ds(LANES * high, LANES)
            out[0, 0:8, comp, span] = piece[8 * high : 8 * high + 8]
            out[0, 8:9, comp, span] = piece[64 + high : 65 + high]


def arrange(received):
    return pl.pallas_call(
        arrange_body,
        out_shape=jax.ShapeDtypeStruct((1, 9, 2, NPH * NDEV), F32),
        compiler_params=params(),
    )(received)


def exchange(values):
    if values.ndim == 3:
        return lax.all_to_all(values, ALL, 0, 0, tiled=True)
    linear = values.reshape(NDEV, 1, values.size // NDEV)
    return lax.all_to_all(linear, ALL, 0, 0, tiled=True).reshape(values.shape)


def shards(
    modes, occup, qprime_coord, shell_vec, target_coord, pair_atoms, block_in, block_out, fc4
):
    picked = exchange(pick(modes, occup, qprime_coord, pair_atoms))
    density = exchange(to_shells(picked, shell_vec))
    renorm = exchange(contract(density, block_in, block_out, fc4))
    delta = exchange(to_targets(renorm, shell_vec, target_coord))
    return arrange(delta).transpose(0, 2, 1, 3)


def solution(mesh):
    return jax.shard_map(
        shards,
        mesh=mesh,
        in_specs=(
            P(("grp", "slab"), None, None, None),
            P(("grp", "slab"), None),
            P(None, ("grp", "slab")),
            P(),
            P(),
            P(),
            P(("grp", "slab")),
            P(("grp", "slab")),
            P(None, ("grp", "slab")),
        ),
        out_specs=P(("grp", "slab"), None, None, None),
        check_vma=False,
    )
```

```python
import math

import jax
import jax.numpy as jnp
import numpy as np
from jax import lax
from jax.experimental import pallas as pl
from jax.experimental.pallas import tpu as pltpu
from jax.sharding import PartitionSpec as P

MESH = 16
LANES = 128
NDEV = 128
NPH = 8
COLS = 72
PITCH = 4 * 384 + 8
FIRST = 5
OTHER = 3
ALL = ("grp", "slab")
F32 = jnp.float32
BF16 = jnp.bfloat16


def params(mebibytes=40):
    return pltpu.CompilerParams(vmem_limit_bytes=mebibytes * 1024 * 1024)


def sixteenth_cos(index):
    wrapped = index - 16.0 * jnp.floor(index * (1.0 / 16.0))
    folded = 4.0 - jnp.minimum(wrapped, 16.0 - wrapped)
    square = folded * folded
    poly = POLY[3]
    for coefficient in (POLY[2], POLY[1], POLY[0]):
        poly = poly * square + coefficient
    return folded * poly


def odd_polynomial():
    points = np.arange(1, 5, dtype=np.float64)
    values = np.sin(np.pi * points / 8.0)
    powers = np.stack([points ** (2 * k + 1) for k in range(4)], 1)
    return [float(c) for c in np.linalg.solve(powers, values)]


POLY = odd_polynomial()


def pick_body(
    coord, atoms, modes, occup, out, held, weights, pairs, spots, points, scaled, rows, dens, picked, sems
):
    copies = [
        pltpu.make_async_copy(occup, weights, sems.at[4]),
        pltpu.make_async_copy(atoms, pairs, sems.at[5]),
        pltpu.make_async_copy(coord, points, sems.at[6]),
    ]
    loads = [pltpu.make_async_copy(modes.at[q], held.at[q], sems.at[q]) for q in range(4)]
    loads[0].start()
    for copy in copies:
        copy.start()
    for load in loads[1:]:
        load.start()
    copies[1].wait()
    first = pairs[0:1, :]
    second = pairs[1:2, :]
    turn = (128 - 3 * (second & 31)) & 127
    pairs[0:1, :] = ((second >> 5) * 384 + first * 3) * 128 + turn
    move = pltpu.make_async_copy(pairs.at[0], spots, sems.at[7])
    move.start()
    copies[0].wait()
    for q in range(4):
        loads[q].wait()
        weight = weights[q : q + 1, :]
        real, imag = held[q, 0], held[q, 1]
        rows[q % 2, 0:384, 0:384] = real
        rows[q % 2, 0:384, 384:768] = imag
        rows[q % 2, 384:768, 0:384] = imag
        rows[q % 2, 384:768, 384:768] = -real
        for part in range(2):
            values = (held[q, part].astype(F32) * weight).astype(BF16)
            for block in range(4):
                scaled[q % 2, 128 * block : 128 * block + 96, pl.ds(384 * part, 384)] = values[
                    96 * block : 96 * block + 96
                ]
        for comp in range(2):
            for half in range(2):
                tile = lax.dot_general(
                    rows[q % 2, 384 * comp : 384 * comp + 384],
                    scaled[q % 2, 256 * half : 256 * half + 256],
                    (((1,), (1,)), ((), ())),
                    preferred_element_type=F32,
                )
                for low in range(2):
                    base = PITCH * (2 * q + comp) + 384 * (2 * half + low)
                    dens[pl.ds(base, 384), :] = tile[:, 128 * low : 128 * low + 128]

    lane = lax.broadcasted_iota(jnp.int32, (8, LANES), 1)
    copies[2].wait()
    move.wait()

    def one(dev, carry):
        acc = jnp.zeros((8, LANES), F32)
        for high in range(NPH):
            spot = spots[high * LANES + dev]
            base = spot >> 7
            for alpha in range(3):
                low = 24 * alpha + 3 * high
                value = dens[pl.ds(base + alpha, 8, stride=PITCH), :]
                turned = pltpu.roll(value, (spot + low) & 127, 1)
                acc = jnp.where((lane >= low) & (lane < low + 3), turned, acc)
        picked[pl.ds(pl.multiple_of(8 * dev, 8), 8), :] = acc
        return carry

    lax.fori_loop(0, NDEV, one, 0, unroll=64)
    lane = lax.broadcasted_iota(jnp.int32, (NDEV, LANES), 1)
    parts = [picked[pl.ds(part, NDEV, stride=8), :] for part in range(8)]
    for part in range(4):
        joined = jnp.where(lane < 64, parts[part], pltpu.roll(parts[part + 4], 64, 1))
        out[pl.ds(part, NDEV, stride=FIRST), :] = joined
    column = lax.broadcasted_iota(jnp.int32, (1, LANES), 1)
    last = jnp.zeros((1, LANES), F32)
    for q in range(4):
        for axis in range(3):
            last = jnp.where(column == 64 + 8 * q + axis, points[axis, q].astype(F32), last)
    last = jnp.broadcast_to(last, (NDEV, LANES))
    for part in range(8):
        piece = pltpu.roll(parts[part], (8 * part + 64) % LANES, 1)
        last = jnp.where((lane >= 8 * part) & (lane < 8 * part + 8), piece, last)
    out[pl.ds(4, NDEV, stride=FIRST), :] = last


def pick(modes, occup, coord, atoms):
    anywhere = pl.BlockSpec(memory_space=pltpu.HBM)
    return pl.pallas_call(
        pick_body,
        in_specs=[anywhere] * 4,
        out_specs=pl.BlockSpec(memory_space=pltpu.VMEM),
        out_shape=jax.ShapeDtypeStruct((NDEV * FIRST, LANES), F32),
        scratch_shapes=[
            pltpu.VMEM((4, 2, 384, 384), BF16),
            pltpu.VMEM((4, 384), F32),
            pltpu.VMEM((2, NPH * LANES), jnp.int32),
            pltpu.SMEM((NPH * LANES,), jnp.int32),
            pltpu.SMEM((3, 4), jnp.int32),
            pltpu.VMEM((2, 512, 768), BF16),
            pltpu.VMEM((2, 768, 768), BF16),
            pltpu.VMEM((PITCH * 8, LANES), F32),
            pltpu.VMEM((8 * NDEV, LANES), F32),
            pltpu.SemaphoreType.DMA((8,)),
        ],
        compiler_params=params(60),
    )(coord, atoms, modes, occup)


def two_parts(values):
    coarse = values.astype(BF16).astype(F32)
    return coarse, values - coarse


def split_dot(left, right):
    left_high, left_low = [part.astype(BF16) for part in two_parts(left)]
    right_high, right_low = [part.astype(BF16) for part in two_parts(right)]
    total = jnp.dot(left_high, right_high, preferred_element_type=F32)
    total = total + jnp.dot(left_high, right_low, preferred_element_type=F32)
    return total + jnp.dot(left_low, right_high, preferred_element_type=F32)


def pack(shells):
    lane = lax.broadcasted_iota(jnp.int32, shells[0].shape, 1)
    return [
        jnp.where(lane < COLS, shells[j], pltpu.roll(shells[3], COLS - 24 * j, 1)) for j in range(3)
    ]


def unpack(rows):
    lane = lax.broadcasted_iota(jnp.int32, rows[0].shape, 1)
    turned = [pltpu.roll(rows[j], LANES - COLS + 24 * j, 1) for j in range(3)]
    last = jnp.where(lane < 24, turned[0], jnp.where(lane < 48, turned[1], turned[2]))
    return [*rows, last]


def shells_body(received, shell, out, summed):
    parts = [received[pl.ds(part, NDEV, stride=FIRST), :] for part in range(FIRST)]
    vector = jnp.concatenate([shell[...].astype(F32), jnp.zeros((5, LANES), F32)], 0)
    vectors = [
        jnp.concatenate(
            [jnp.zeros((64 + 8 * q, LANES), F32), vector, jnp.zeros((56 - 8 * q, LANES), F32)], 0
        )
        for q in range(4)
    ]
    index = lax.dot_general(
        jnp.concatenate(vectors, 1),
        parts[4],
        (((0,), (1,)), ((), ())),
        preferred_element_type=F32,
    )
    waves = [sixteenth_cos(index), sixteenth_cos(index + 4.0)]
    waves = [waves[part % 2][LANES * (part // 2) : LANES * (part // 2 + 1)] for part in range(8)]
    lane = lax.broadcasted_iota(jnp.int32, (NDEV, LANES), 1)
    values = []
    for part in range(8):
        main = parts[part] if part < 4 else pltpu.roll(parts[part - 4], 64, 1)
        rest = pltpu.roll(parts[4], (64 - 8 * part) % LANES, 1)
        values.append(jnp.where(lane < 64, main, rest))
    rho = split_dot(jnp.concatenate(waves, 1), jnp.concatenate(values, 0))
    summed[...] = rho * (1.0 / math.sqrt(512.0))
    rows = pack([summed[pl.ds(low, 32, stride=4), :] for low in range(4)])
    for j in range(3):
        for group in range(4):
            out[pl.ds(OTHER * 32 * group + j, 32, stride=OTHER), :] = rows[j]


def to_shells(received, shell):
    return pl.pallas_call(
        shells_body,
        out_shape=jax.ShapeDtypeStruct((NDEV * OTHER, LANES), F32),
        scratch_shapes=[pltpu.VMEM((LANES, LANES), F32)],
        compiler_params=params(),
    )(received, shell)


def block_tables():
    column = np.arange(2 * COLS)
    rest = column % COLS
    comp = 3 * (rest // 24) + rest % 3
    level = 8 * (column // COLS) + (rest % 24) // 3
    row = np.where(comp < 8, 8 * level + comp, 128 + level)
    return (np.arange(2 * COLS)[:, None] == row[None, :]).astype(np.float32)


def contract_body(
    chunk, unroll, received, place, reads, writes, fc4, out, table, total, terms
):
    shells = unpack([received[pl.ds(j, NDEV, stride=OTHER), :] for j in range(3)])
    for high in range(2):
        pieces = [shells[2 * high + low][:, :COLS] for low in range(2)]
        parts = jnp.concatenate(two_parts(jnp.concatenate(pieces, 1)), 0).astype(BF16)
        turned = lax.dot_general(
            place[...].astype(BF16),
            parts,
            (((1,), (1,)), ((), ())),
            preferred_element_type=F32,
        ).astype(BF16)
        span = pl.ds(high * LANES, LANES)
        table[0:144, span] = turned[:, :LANES]
        table[144:288, span] = turned[:, LANES:]
    total[...] = jnp.zeros_like(total)
    level = lax.broadcasted_iota(jnp.int32, (16, chunk), 0)
    level_pair = (level >> 3).astype(BF16)
    level_all = level.astype(BF16)
    low_place = lax.broadcasted_iota(jnp.int32, (2 * LANES, chunk), 0).astype(BF16)
    unit, zero = jnp.ones((), BF16), jnp.zeros((), BF16)

    def small(values):
        return values.astype(F32).astype(BF16)

    def low_hot(entry):
        low = ((entry >> 11) << 7) | (entry & 127)
        return jnp.where(low_place == small(low), unit, zero)

    def one(step, carry):
        span = pl.ds(pl.multiple_of(step * chunk, chunk), chunk)
        for block in range(chunk // LANES):
            part = pl.ds(pl.multiple_of(step * chunk + block * LANES, LANES), LANES)
            terms[block, 0:81, :] = fc4[:, part].astype(F32)

        def term(start, count, stride=1):
            rows = pl.ds(start, count, stride=stride)
            return jnp.concatenate(
                [terms[block, rows, :] for block in range(chunk // LANES)], 1
            )

        read, write = reads[:, span], writes[:, span]
        read_high = (read >> 7) & 15
        write_high = small((write >> 7) & 15)
        found = jnp.dot(table[...], low_hot(read), preferred_element_type=F32)
        found = found[:144] + found[144:]
        main = found[0:8]
        for high in range(1, 16):
            main = jnp.where(read_high == high, found[8 * high : 8 * high + 8], main)
        last = jnp.sum(jnp.where(level == read_high, found[128:144], 0.0), 0, keepdims=True)
        contrib = term(8, 8, 9) * last
        for comp in range(8):
            contrib = contrib + term(comp, 8, 9) * main[comp : comp + 1]
        ninth = jnp.sum(term(72, 8) * main, 0, keepdims=True) + term(80, 1) * last
        spread = []
        for body, tail in zip(two_parts(contrib), two_parts(ninth)):
            body = jnp.concatenate([body, body], 0).astype(BF16)
            tail = jnp.broadcast_to(tail, level.shape).astype(BF16)
            for pair in range(8):
                spread.append(jnp.where(level_pair + 2 * pair == write_high, body, zero))
            spread.append(jnp.where(level_all == write_high, tail, zero))
        added = lax.dot_general(
            jnp.concatenate(spread, 0),
            low_hot(write),
            (((1,), (1,)), ((), ())),
            preferred_element_type=F32,
        )
        for high in range(2):
            total[high] += added[:, high * LANES : high * LANES + LANES]
        return carry

    lax.fori_loop(0, fc4.shape[1] // chunk, one, 0, unroll=unroll)
    shells = []
    for shell in range(4):
        low, high = shell % 2, shell // 2
        rows = []
        for comp in range(9):
            start = 64 * low + comp if comp < 8 else 128 + 8 * low
            stride = 8 if comp < 8 else 1
            rows.append(
                total[high, pl.ds(start, 8, stride=stride), :]
                + total[high, pl.ds(144 + start, 8, stride=stride), :]
            )
        rows.append(jnp.zeros((LANES - COLS, LANES), F32))
        shells.append(jnp.concatenate(rows, 0).T)
    for j, row in enumerate(pack(shells)):
        out[pl.ds(j, NDEV, stride=OTHER), :] = row


def contract(received, block_in, block_out, fc4, chunk=16384, unroll=1):
    nblocks = fc4.shape[1]
    place = block_tables()
    reads, writes = block_in.reshape(1, nblocks), block_out.reshape(1, nblocks)

    def body(*refs):
        contract_body(chunk, unroll, *refs)

    return pl.pallas_call(
        body,
        out_shape=jax.ShapeDtypeStruct((NDEV * OTHER, LANES), F32),
        scratch_shapes=[
            pltpu.VMEM((4 * COLS, 2 * LANES), BF16),
            pltpu.VMEM((2, 4 * COLS, LANES), F32),
            pltpu.VMEM((chunk // LANES, 88, LANES), F32),
        ],
        compiler_params=params(48),
    )(received, jnp.asarray(place), reads, writes, fc4)


def targets_body(received, shell, target, out):
    rows = []
    for j in range(3):
        piece = received[pl.ds(j, NDEV, stride=OTHER), :]
        rows.append(piece[0:32] + piece[32:64] + piece[64:96] + piece[96:128])
    renorm = jnp.concatenate(unpack(rows), 0)
    source = lax.broadcasted_iota(jnp.int32, (LANES, LANES), 0)
    order = lax.broadcasted_iota(jnp.int32, (LANES, LANES), 1)
    order = jnp.where(source == (order % 32) * 4 + order // 32, 1.0, 0.0)
    pad = jnp.zeros((5, LANES), F32)
    vectors = jnp.concatenate([shell[...].astype(F32), pad], 0)
    points = jnp.concatenate([target[...].astype(F32), pad], 0)
    vectors = jnp.dot(vectors, order, preferred_element_type=F32)
    index = lax.dot_general(
        points, vectors, (((0,), (0,)), ((), ())), preferred_element_type=F32
    )
    out[pl.ds(0, NDEV, stride=2), :] = split_dot(sixteenth_cos(index), renorm)
    out[pl.ds(1, NDEV, stride=2), :] = split_dot(sixteenth_cos(index + 4.0), renorm)


def to_targets(received, shell, target):
    return pl.pallas_call(
        targets_body,
        out_shape=jax.ShapeDtypeStruct((NDEV * 2, LANES), F32),
        compiler_params=params(),
    )(received, shell, target)


def arrange_body(received, out):
    for comp in range(2):
        turned = received[pl.ds(comp, NDEV, stride=2), :].T
        out[pl.ds(comp, COLS, stride=2), :] = turned[:COLS]


def arrange(received):
    rows = pl.pallas_call(
        arrange_body,
        out_shape=jax.ShapeDtypeStruct((2 * COLS, LANES), F32),
        compiler_params=params(),
    )(received)
    rows = rows.reshape(9, NPH, 2, LANES).transpose(2, 0, 1, 3)
    return rows.reshape(1, 2, 9, NPH * LANES)


def exchange(values):
    linear = values.reshape(NDEV, 1, values.size // NDEV)
    return lax.all_to_all(linear, ALL, 0, 0, tiled=True).reshape(values.shape)


def shards(
    modes, occup, qprime_coord, shell_vec, target_coord, pair_atoms, block_in, block_out, fc4
):
    picked = exchange(pick(modes, occup, qprime_coord, pair_atoms))
    density = exchange(to_shells(picked, shell_vec))
    renorm = exchange(contract(density, block_in, block_out, fc4))
    delta = exchange(to_targets(renorm, shell_vec, target_coord))
    return arrange(delta)


def solution(mesh):
    return jax.shard_map(
        shards,
        mesh=mesh,
        in_specs=(
            P(("grp", "slab"), None, None, None),
            P(("grp", "slab"), None),
            P(None, ("grp", "slab")),
            P(),
            P(),
            P(),
            P(("grp", "slab")),
            P(("grp", "slab")),
            P(None, ("grp", "slab")),
        ),
        out_specs=P(("grp", "slab"), None, None, None),
        check_vma=False,
    )
```

```python
import math

import jax
import jax.numpy as jnp
import numpy as np
from jax import lax
from jax.experimental import pallas as pl
from jax.experimental.pallas import tpu as pltpu
from jax.sharding import PartitionSpec as P

MESH = 16
LANES = 128
NDEV = 128
NPH = 8
COLS = 72
PITCH = 4 * 384 + 8
FIRST = 5
OTHER = 3
ALL = ("grp", "slab")
F32 = jnp.float32
BF16 = jnp.bfloat16


def params(mebibytes=40):
    return pltpu.CompilerParams(vmem_limit_bytes=mebibytes * 1024 * 1024)


def sixteenth_cos(index):
    wrapped = index - 16.0 * jnp.floor(index * (1.0 / 16.0))
    folded = 4.0 - jnp.minimum(wrapped, 16.0 - wrapped)
    square = folded * folded
    poly = POLY[3]
    for coefficient in (POLY[2], POLY[1], POLY[0]):
        poly = poly * square + coefficient
    return folded * poly


def odd_polynomial():
    points = np.arange(1, 5, dtype=np.float64)
    values = np.sin(np.pi * points / 8.0)
    powers = np.stack([points ** (2 * k + 1) for k in range(4)], 1)
    return [float(c) for c in np.linalg.solve(powers, values)]


POLY = odd_polynomial()


def pick_body(
    coord, atoms, modes, occup, out, held, weights, pairs, spots, points, scaled, rows, dens, picked, sems
):
    copies = [
        pltpu.make_async_copy(occup, weights, sems.at[4]),
        pltpu.make_async_copy(atoms, pairs, sems.at[5]),
        pltpu.make_async_copy(coord, points, sems.at[6]),
    ]
    loads = [pltpu.make_async_copy(modes.at[q], held.at[q], sems.at[q]) for q in range(4)]
    loads[0].start()
    for copy in copies:
        copy.start()
    for load in loads[1:]:
        load.start()
    copies[1].wait()
    first = pairs[0:1, :]
    second = pairs[1:2, :]
    turn = (128 - 3 * (second & 31)) & 127
    pairs[0:1, :] = ((second >> 5) * 384 + first * 3) * 128 + turn
    move = pltpu.make_async_copy(pairs.at[0], spots, sems.at[7])
    move.start()
    copies[0].wait()
    for q in range(4):
        loads[q].wait()
        weight = weights[q : q + 1, :]
        real, imag = held[q, 0], held[q, 1]
        rows[q % 2, 0:384, 0:384] = real
        rows[q % 2, 0:384, 384:768] = imag
        rows[q % 2, 384:768, 0:384] = imag
        rows[q % 2, 384:768, 384:768] = -real
        for part in range(2):
            values = (held[q, part].astype(F32) * weight).astype(BF16)
            for block in range(4):
                scaled[q % 2, 128 * block : 128 * block + 96, pl.ds(384 * part, 384)] = values[
                    96 * block : 96 * block + 96
                ]
        for comp in range(2):
            for half in range(2):
                tile = lax.dot_general(
                    rows[q % 2, 384 * comp : 384 * comp + 384],
                    scaled[q % 2, 256 * half : 256 * half + 256],
                    (((1,), (1,)), ((), ())),
                    preferred_element_type=F32,
                )
                for low in range(2):
                    base = PITCH * (2 * q + comp) + 384 * (2 * half + low)
                    dens[pl.ds(base, 384), :] = tile[:, 128 * low : 128 * low + 128]

    slot = lax.broadcasted_iota(jnp.int32, (8, LANES), 1) // 3
    copies[2].wait()
    move.wait()

    def one(dev, carry):
        acc = jnp.zeros((8, LANES), F32)
        for high in range(NPH):
            spot = spots[high * LANES + dev]
            base = spot >> 7
            for alpha in range(3):
                low = 24 * alpha + 3 * high
                value = dens[pl.ds(base + alpha, 8, stride=PITCH), :]
                turned = pltpu.roll(value, (spot + low) & 127, 1)
                acc = jnp.where(slot == low // 3, turned, acc)
        picked[pl.ds(pl.multiple_of(8 * dev, 8), 8), :] = acc
        return carry

    lax.fori_loop(0, NDEV, one, 0, unroll=128)
    lane = lax.broadcasted_iota(jnp.int32, (NDEV, LANES), 1)
    parts = [picked[pl.ds(part, NDEV, stride=8), :] for part in range(8)]
    for part in range(4):
        joined = jnp.where(lane < 64, parts[part], pltpu.roll(parts[part + 4], 64, 1))
        out[pl.ds(part, NDEV, stride=FIRST), :] = joined
    column = lax.broadcasted_iota(jnp.int32, (1, LANES), 1)
    last = jnp.zeros((1, LANES), F32)
    for q in range(4):
        for axis in range(3):
            last = jnp.where(column == 64 + 8 * q + axis, points[axis, q].astype(F32), last)
    last = jnp.broadcast_to(last, (NDEV, LANES))
    for part in range(8):
        piece = pltpu.roll(parts[part], (8 * part + 64) % LANES, 1)
        last = jnp.where((lane >= 8 * part) & (lane < 8 * part + 8), piece, last)
    out[pl.ds(4, NDEV, stride=FIRST), :] = last


def pick(modes, occup, coord, atoms):
    anywhere = pl.BlockSpec(memory_space=pltpu.HBM)
    return pl.pallas_call(
        pick_body,
        in_specs=[anywhere] * 4,
        out_specs=pl.BlockSpec(memory_space=pltpu.VMEM),
        out_shape=jax.ShapeDtypeStruct((NDEV * FIRST, LANES), F32),
        scratch_shapes=[
            pltpu.VMEM((4, 2, 384, 384), BF16),
            pltpu.VMEM((4, 384), F32),
            pltpu.VMEM((2, NPH * LANES), jnp.int32),
            pltpu.SMEM((NPH * LANES,), jnp.int32),
            pltpu.SMEM((3, 4), jnp.int32),
            pltpu.VMEM((2, 512, 768), BF16),
            pltpu.VMEM((2, 768, 768), BF16),
            pltpu.VMEM((PITCH * 9, LANES), F32),
            pltpu.VMEM((8 * NDEV, LANES), F32),
            pltpu.SemaphoreType.DMA((8,)),
        ],
        compiler_params=params(60),
    )(coord, atoms, modes, occup)


def two_parts(values):
    coarse = values.astype(BF16).astype(F32)
    return coarse, values - coarse


def split_dot(left, right):
    left_high, left_low = [part.astype(BF16) for part in two_parts(left)]
    right_high, right_low = [part.astype(BF16) for part in two_parts(right)]
    total = jnp.dot(left_high, right_high, preferred_element_type=F32)
    total = total + jnp.dot(left_high, right_low, preferred_element_type=F32)
    return total + jnp.dot(left_low, right_high, preferred_element_type=F32)


def pack(shells):
    lane = lax.broadcasted_iota(jnp.int32, shells[0].shape, 1)
    return [
        jnp.where(lane < COLS, shells[j], pltpu.roll(shells[3], COLS - 24 * j, 1)) for j in range(3)
    ]


def unpack(rows):
    lane = lax.broadcasted_iota(jnp.int32, rows[0].shape, 1)
    turned = [pltpu.roll(rows[j], LANES - COLS + 24 * j, 1) for j in range(3)]
    last = jnp.where(lane < 24, turned[0], jnp.where(lane < 48, turned[1], turned[2]))
    return [*rows, last]


def shells_body(received, shell, out, summed):
    parts = [received[pl.ds(part, NDEV, stride=FIRST), :] for part in range(FIRST)]
    vector = jnp.concatenate([shell[...].astype(F32), jnp.zeros((5, LANES), F32)], 0)
    vectors = [
        jnp.concatenate(
            [jnp.zeros((64 + 8 * q, LANES), F32), vector, jnp.zeros((56 - 8 * q, LANES), F32)], 0
        )
        for q in range(4)
    ]
    index = lax.dot_general(
        jnp.concatenate(vectors, 1),
        parts[4],
        (((0,), (1,)), ((), ())),
        preferred_element_type=F32,
    )
    waves = [sixteenth_cos(index), sixteenth_cos(index + 4.0)]
    waves = [waves[part % 2][LANES * (part // 2) : LANES * (part // 2 + 1)] for part in range(8)]
    lane = lax.broadcasted_iota(jnp.int32, (NDEV, LANES), 1)
    values = []
    for part in range(8):
        main = parts[part] if part < 4 else pltpu.roll(parts[part - 4], 64, 1)
        rest = pltpu.roll(parts[4], (64 - 8 * part) % LANES, 1)
        values.append(jnp.where(lane < 64, main, rest))
    rho = split_dot(jnp.concatenate(waves, 1), jnp.concatenate(values, 0))
    summed[...] = rho * (1.0 / math.sqrt(512.0))
    rows = pack([summed[pl.ds(low, 32, stride=4), :] for low in range(4)])
    for j in range(3):
        for group in range(4):
            out[pl.ds(OTHER * 32 * group + j, 32, stride=OTHER), :] = rows[j]


def to_shells(received, shell):
    return pl.pallas_call(
        shells_body,
        out_shape=jax.ShapeDtypeStruct((NDEV * OTHER, LANES), F32),
        scratch_shapes=[pltpu.VMEM((LANES, LANES), F32)],
        compiler_params=params(),
    )(received, shell)


def block_tables():
    column = np.arange(2 * COLS)
    rest = column % COLS
    comp = 3 * (rest // 24) + rest % 3
    level = 8 * (column // COLS) + (rest % 24) // 3
    row = np.where(comp < 8, 8 * level + comp, 128 + level)
    return (np.arange(2 * COLS)[:, None] == row[None, :]).astype(np.float32)


def contract_body(
    chunk, unroll, received, place, reads, writes, fc4, out, table, total, terms
):
    shells = unpack([received[pl.ds(j, NDEV, stride=OTHER), :] for j in range(3)])
    for high in range(2):
        pieces = [shells[2 * high + low][:, :COLS] for low in range(2)]
        parts = jnp.concatenate(two_parts(jnp.concatenate(pieces, 1)), 0).astype(BF16)
        turned = lax.dot_general(
            place[...].astype(BF16),
            parts,
            (((1,), (1,)), ((), ())),
            preferred_element_type=F32,
        ).astype(BF16)
        span = pl.ds(high * LANES, LANES)
        table[0:144, span] = turned[:, :LANES]
        table[144:288, span] = turned[:, LANES:]
    total[...] = jnp.zeros_like(total)
    level = lax.broadcasted_iota(jnp.int32, (16, chunk), 0)
    level_pair = (level >> 3).astype(BF16)
    level_all = level.astype(BF16)
    low_place = lax.broadcasted_iota(jnp.int32, (2 * LANES, chunk), 0).astype(BF16)
    unit, zero = jnp.ones((), BF16), jnp.zeros((), BF16)

    def small(values):
        return values.astype(F32).astype(BF16)

    def low_hot(entry):
        low = ((entry >> 11) << 7) | (entry & 127)
        return jnp.where(low_place == small(low), unit, zero)

    def one(step, carry):
        span = pl.ds(pl.multiple_of(step * chunk, chunk), chunk)
        for block in range(chunk // LANES):
            part = pl.ds(pl.multiple_of(step * chunk + block * LANES, LANES), LANES)
            terms[block, 0:81, :] = fc4[:, part].astype(F32)

        def term(start, count, stride=1):
            rows = pl.ds(start, count, stride=stride)
            return jnp.concatenate(
                [terms[block, rows, :] for block in range(chunk // LANES)], 1
            )

        read, write = reads[:, span], writes[:, span]
        read_high = (read >> 7) & 15
        write_high = small((write >> 7) & 15)
        found = jnp.dot(table[...], low_hot(read), preferred_element_type=F32)
        found = found[:144] + found[144:]
        main = found[0:8]
        for high in range(1, 16):
            main = jnp.where(read_high == high, found[8 * high : 8 * high + 8], main)
        last = jnp.sum(jnp.where(level == read_high, found[128:144], 0.0), 0, keepdims=True)
        contrib = term(8, 8, 9) * last
        for comp in range(8):
            contrib = contrib + term(comp, 8, 9) * main[comp : comp + 1]
        ninth = jnp.sum(term(72, 8) * main, 0, keepdims=True) + term(80, 1) * last
        spread = []
        for body, tail in zip(two_parts(contrib), two_parts(ninth)):
            body = jnp.concatenate([body, body], 0).astype(BF16)
            tail = jnp.broadcast_to(tail, level.shape).astype(BF16)
            for pair in range(8):
                spread.append(jnp.where(level_pair + 2 * pair == write_high, body, zero))
            spread.append(jnp.where(level_all == write_high, tail, zero))
        added = lax.dot_general(
            jnp.concatenate(spread, 0),
            low_hot(write),
            (((1,), (1,)), ((), ())),
            preferred_element_type=F32,
        )
        for high in range(2):
            total[high] += added[:, high * LANES : high * LANES + LANES]
        return carry

    lax.fori_loop(0, fc4.shape[1] // chunk, one, 0, unroll=unroll)
    shells = []
    for shell in range(4):
        low, high = shell % 2, shell // 2
        rows = []
        for comp in range(9):
            start = 64 * low + comp if comp < 8 else 128 + 8 * low
            stride = 8 if comp < 8 else 1
            rows.append(
                total[high, pl.ds(start, 8, stride=stride), :]
                + total[high, pl.ds(144 + start, 8, stride=stride), :]
            )
        rows.append(jnp.zeros((LANES - COLS, LANES), F32))
        shells.append(jnp.concatenate(rows, 0).T)
    for j, row in enumerate(pack(shells)):
        out[pl.ds(j, NDEV, stride=OTHER), :] = row


def contract(received, block_in, block_out, fc4, chunk=16384, unroll=1):
    nblocks = fc4.shape[1]
    place = block_tables()
    reads, writes = block_in.reshape(1, nblocks), block_out.reshape(1, nblocks)

    def body(*refs):
        contract_body(chunk, unroll, *refs)

    return pl.pallas_call(
        body,
        out_shape=jax.ShapeDtypeStruct((NDEV * OTHER, LANES), F32),
        scratch_shapes=[
            pltpu.VMEM((4 * COLS, 2 * LANES), BF16),
            pltpu.VMEM((2, 4 * COLS, LANES), F32),
            pltpu.VMEM((chunk // LANES, 88, LANES), F32),
        ],
        compiler_params=params(48),
    )(received, jnp.asarray(place), reads, writes, fc4)


def targets_body(received, shell, target, out):
    rows = []
    for j in range(3):
        piece = received[pl.ds(j, NDEV, stride=OTHER), :]
        rows.append(piece[0:32] + piece[32:64] + piece[64:96] + piece[96:128])
    renorm = jnp.concatenate(unpack(rows), 0)
    source = lax.broadcasted_iota(jnp.int32, (LANES, LANES), 0)
    order = lax.broadcasted_iota(jnp.int32, (LANES, LANES), 1)
    order = jnp.where(source == (order % 32) * 4 + order // 32, 1.0, 0.0)
    pad = jnp.zeros((5, LANES), F32)
    vectors = jnp.concatenate([shell[...].astype(F32), pad], 0)
    points = jnp.concatenate([target[...].astype(F32), pad], 0)
    vectors = jnp.dot(vectors, order, preferred_element_type=F32)
    index = lax.dot_general(
        points, vectors, (((0,), (0,)), ((), ())), preferred_element_type=F32
    )
    out[pl.ds(0, NDEV, stride=2), :] = split_dot(sixteenth_cos(index), renorm)
    out[pl.ds(1, NDEV, stride=2), :] = split_dot(sixteenth_cos(index + 4.0), renorm)


def to_targets(received, shell, target):
    return pl.pallas_call(
        targets_body,
        out_shape=jax.ShapeDtypeStruct((NDEV * 2, LANES), F32),
        compiler_params=params(),
    )(received, shell, target)


def arrange_body(received, out):
    for comp in range(2):
        turned = received[pl.ds(comp, NDEV, stride=2), :].T
        out[pl.ds(comp, COLS, stride=2), :] = turned[:COLS]


def arrange(received):
    rows = pl.pallas_call(
        arrange_body,
        out_shape=jax.ShapeDtypeStruct((2 * COLS, LANES), F32),
        compiler_params=params(),
    )(received)
    rows = rows.reshape(9, NPH, 2, LANES).transpose(2, 0, 1, 3)
    return rows.reshape(1, 2, 9, NPH * LANES)


def exchange(values):
    linear = values.reshape(NDEV, 1, values.size // NDEV)
    return lax.all_to_all(linear, ALL, 0, 0, tiled=True).reshape(values.shape)


def shards(
    modes, occup, qprime_coord, shell_vec, target_coord, pair_atoms, block_in, block_out, fc4
):
    picked = exchange(pick(modes, occup, qprime_coord, pair_atoms))
    density = exchange(to_shells(picked, shell_vec))
    renorm = exchange(contract(density, block_in, block_out, fc4))
    delta = exchange(to_targets(renorm, shell_vec, target_coord))
    return arrange(delta)


def solution(mesh):
    return jax.shard_map(
        shards,
        mesh=mesh,
        in_specs=(
            P(("grp", "slab"), None, None, None),
            P(("grp", "slab"), None),
            P(None, ("grp", "slab")),
            P(),
            P(),
            P(),
            P(("grp", "slab")),
            P(("grp", "slab")),
            P(None, ("grp", "slab")),
        ),
        out_specs=P(("grp", "slab"), None, None, None),
        check_vma=False,
    )
```

```python
import math

import jax
import jax.numpy as jnp
import numpy as np
from jax import lax
from jax.experimental import pallas as pl
from jax.experimental.pallas import tpu as pltpu
from jax.sharding import PartitionSpec as P

MESH = 16
LANES = 128
NDEV = 128
NPH = 8
COLS = 72
PITCH = 4 * 384 + 8
FIRST = 5
OTHER = 3
ALL = ("grp", "slab")
F32 = jnp.float32
BF16 = jnp.bfloat16


def params(mebibytes=40):
    return pltpu.CompilerParams(vmem_limit_bytes=mebibytes * 1024 * 1024)


def sixteenth_cos(index):
    wrapped = index - 16.0 * jnp.floor(index * (1.0 / 16.0))
    folded = 4.0 - jnp.minimum(wrapped, 16.0 - wrapped)
    square = folded * folded
    poly = POLY[3]
    for coefficient in (POLY[2], POLY[1], POLY[0]):
        poly = poly * square + coefficient
    return folded * poly


def odd_polynomial():
    points = np.arange(1, 5, dtype=np.float64)
    values = np.sin(np.pi * points / 8.0)
    powers = np.stack([points ** (2 * k + 1) for k in range(4)], 1)
    return [float(c) for c in np.linalg.solve(powers, values)]


POLY = odd_polynomial()


def pick_body(
    coord, atoms, modes, occup, out, held, weights, pairs, spots, points, scaled, rows, dens, picked, sems
):
    copies = [
        pltpu.make_async_copy(occup, weights, sems.at[4]),
        pltpu.make_async_copy(atoms, pairs, sems.at[5]),
        pltpu.make_async_copy(coord, points, sems.at[6]),
    ]
    loads = [pltpu.make_async_copy(modes.at[q], held.at[q], sems.at[q]) for q in range(4)]
    loads[0].start()
    for copy in copies:
        copy.start()
    for load in loads[1:]:
        load.start()
    copies[1].wait()
    first = pairs[0:1, :]
    second = pairs[1:2, :]
    turn = (128 - 3 * (second & 31)) & 127
    pairs[0:1, :] = ((second >> 5) * 384 + first * 3) * 128 + turn
    move = pltpu.make_async_copy(pairs.at[0], spots, sems.at[7])
    move.start()
    copies[0].wait()
    for q in range(4):
        loads[q].wait()
        weight = weights[q : q + 1, :]
        real, imag = held[q, 0], held[q, 1]
        rows[q % 2, 0:384, 0:384] = real
        rows[q % 2, 0:384, 384:768] = imag
        rows[q % 2, 384:768, 0:384] = imag
        rows[q % 2, 384:768, 384:768] = -real
        for part in range(2):
            values = (held[q, part].astype(F32) * weight).astype(BF16)
            for block in range(4):
                scaled[q % 2, 128 * block : 128 * block + 96, pl.ds(384 * part, 384)] = values[
                    96 * block : 96 * block + 96
                ]
        for comp in range(2):
            for half in range(2):
                tile = lax.dot_general(
                    rows[q % 2, 384 * comp : 384 * comp + 384],
                    scaled[q % 2, 256 * half : 256 * half + 256],
                    (((1,), (1,)), ((), ())),
                    preferred_element_type=F32,
                )
                for low in range(2):
                    base = PITCH * (2 * q + comp) + 384 * (2 * half + low)
                    dens[pl.ds(base, 384), :] = tile[:, 128 * low : 128 * low + 128]

    slot = lax.broadcasted_iota(jnp.int32, (8, LANES), 1) // 3
    copies[2].wait()
    move.wait()

    def one(dev, carry):
        acc = jnp.zeros((8, LANES), F32)
        for high in range(NPH):
            spot = spots[high * LANES + dev]
            base = spot >> 7
            for alpha in range(3):
                low = 24 * alpha + 3 * high
                value = dens[pl.ds(base + alpha, 8, stride=PITCH), :]
                turned = pltpu.roll(value, (spot + low) & 127, 1)
                acc = jnp.where(slot == low // 3, turned, acc)
        picked[pl.ds(pl.multiple_of(8 * dev, 8), 8), :] = acc
        return carry

    lax.fori_loop(0, NDEV, one, 0, unroll=128)
    lane = lax.broadcasted_iota(jnp.int32, (NDEV, LANES), 1)
    parts = [picked[pl.ds(part, NDEV, stride=8), :] for part in range(8)]
    for part in range(4):
        joined = jnp.where(lane < 64, parts[part], pltpu.roll(parts[part + 4], 64, 1))
        out[pl.ds(part, NDEV, stride=FIRST), :] = joined
    column = lax.broadcasted_iota(jnp.int32, (1, LANES), 1)
    last = jnp.zeros((1, LANES), F32)
    for q in range(4):
        for axis in range(3):
            last = jnp.where(column == 64 + 8 * q + axis, points[axis, q].astype(F32), last)
    last = jnp.broadcast_to(last, (NDEV, LANES))
    for part in range(8):
        piece = pltpu.roll(parts[part], (8 * part + 64) % LANES, 1)
        last = jnp.where((lane >= 8 * part) & (lane < 8 * part + 8), piece, last)
    out[pl.ds(4, NDEV, stride=FIRST), :] = last


def pick(modes, occup, coord, atoms):
    anywhere = pl.BlockSpec(memory_space=pltpu.HBM)
    return pl.pallas_call(
        pick_body,
        in_specs=[anywhere] * 4,
        out_specs=pl.BlockSpec(memory_space=pltpu.VMEM),
        out_shape=pltpu.VMEM((NDEV * FIRST, LANES), F32),
        scratch_shapes=[
            pltpu.VMEM((4, 2, 384, 384), BF16),
            pltpu.VMEM((4, 384), F32),
            pltpu.VMEM((2, NPH * LANES), jnp.int32),
            pltpu.SMEM((NPH * LANES,), jnp.int32),
            pltpu.SMEM((3, 4), jnp.int32),
            pltpu.VMEM((2, 512, 768), BF16),
            pltpu.VMEM((2, 768, 768), BF16),
            pltpu.VMEM((PITCH * 9, LANES), F32),
            pltpu.VMEM((8 * NDEV, LANES), F32),
            pltpu.SemaphoreType.DMA((8,)),
        ],
        compiler_params=params(60),
    )(coord, atoms, modes, occup)


def two_parts(values):
    coarse = values.astype(BF16).astype(F32)
    return coarse, values - coarse


def split_dot(left, right):
    left_high, left_low = [part.astype(BF16) for part in two_parts(left)]
    right_high, right_low = [part.astype(BF16) for part in two_parts(right)]
    total = jnp.dot(left_high, right_high, preferred_element_type=F32)
    total = total + jnp.dot(left_high, right_low, preferred_element_type=F32)
    return total + jnp.dot(left_low, right_high, preferred_element_type=F32)


def pack(shells):
    lane = lax.broadcasted_iota(jnp.int32, shells[0].shape, 1)
    return [
        jnp.where(lane < COLS, shells[j], pltpu.roll(shells[3], COLS - 24 * j, 1)) for j in range(3)
    ]


def unpack(rows):
    lane = lax.broadcasted_iota(jnp.int32, rows[0].shape, 1)
    turned = [pltpu.roll(rows[j], LANES - COLS + 24 * j, 1) for j in range(3)]
    last = jnp.where(lane < 24, turned[0], jnp.where(lane < 48, turned[1], turned[2]))
    return [*rows, last]


def shells_body(received, shell, out, summed):
    parts = [received[pl.ds(part, NDEV, stride=FIRST), :] for part in range(FIRST)]
    vector = jnp.concatenate([shell[...].astype(F32), jnp.zeros((5, LANES), F32)], 0)
    vectors = [
        jnp.concatenate(
            [jnp.zeros((64 + 8 * q, LANES), F32), vector, jnp.zeros((56 - 8 * q, LANES), F32)], 0
        )
        for q in range(4)
    ]
    index = lax.dot_general(
        jnp.concatenate(vectors, 1),
        parts[4],
        (((0,), (1,)), ((), ())),
        preferred_element_type=F32,
    )
    waves = [sixteenth_cos(index), sixteenth_cos(index + 4.0)]
    waves = [waves[part % 2][LANES * (part // 2) : LANES * (part // 2 + 1)] for part in range(8)]
    lane = lax.broadcasted_iota(jnp.int32, (NDEV, LANES), 1)
    values = []
    for part in range(8):
        main = parts[part] if part < 4 else pltpu.roll(parts[part - 4], 64, 1)
        rest = pltpu.roll(parts[4], (64 - 8 * part) % LANES, 1)
        values.append(jnp.where(lane < 64, main, rest))
    rho = split_dot(jnp.concatenate(waves, 1), jnp.concatenate(values, 0))
    summed[...] = rho * (1.0 / math.sqrt(512.0))
    rows = pack([summed[pl.ds(low, 32, stride=4), :] for low in range(4)])
    for j in range(3):
        for group in range(4):
            out[pl.ds(OTHER * 32 * group + j, 32, stride=OTHER), :] = rows[j]


def to_shells(received, shell):
    return pl.pallas_call(
        shells_body,
        out_shape=jax.ShapeDtypeStruct((NDEV * OTHER, LANES), F32),
        scratch_shapes=[pltpu.VMEM((LANES, LANES), F32)],
        compiler_params=params(),
    )(received, shell)


def block_tables():
    column = np.arange(2 * COLS)
    rest = column % COLS
    comp = 3 * (rest // 24) + rest % 3
    level = 8 * (column // COLS) + (rest % 24) // 3
    row = np.where(comp < 8, 8 * level + comp, 128 + level)
    return (np.arange(2 * COLS)[:, None] == row[None, :]).astype(np.float32)


def contract_body(
    chunk, unroll, received, place, reads, writes, fc4, out, table, total, terms
):
    shells = unpack([received[pl.ds(j, NDEV, stride=OTHER), :] for j in range(3)])
    for high in range(2):
        pieces = [shells[2 * high + low][:, :COLS] for low in range(2)]
        parts = jnp.concatenate(two_parts(jnp.concatenate(pieces, 1)), 0).astype(BF16)
        turned = lax.dot_general(
            place[...].astype(BF16),
            parts,
            (((1,), (1,)), ((), ())),
            preferred_element_type=F32,
        ).astype(BF16)
        span = pl.ds(high * LANES, LANES)
        table[0:144, span] = turned[:, :LANES]
        table[144:288, span] = turned[:, LANES:]
    total[...] = jnp.zeros_like(total)
    level = lax.broadcasted_iota(jnp.int32, (16, chunk), 0)
    level_pair = (level >> 3).astype(BF16)
    level_all = level.astype(BF16)
    low_place = lax.broadcasted_iota(jnp.int32, (2 * LANES, chunk), 0).astype(BF16)
    unit, zero = jnp.ones((), BF16), jnp.zeros((), BF16)

    def small(values):
        return values.astype(F32).astype(BF16)

    def low_hot(entry):
        low = ((entry >> 11) << 7) | (entry & 127)
        return jnp.where(low_place == small(low), unit, zero)

    def one(step, carry):
        span = pl.ds(pl.multiple_of(step * chunk, chunk), chunk)
        for block in range(chunk // LANES):
            part = pl.ds(pl.multiple_of(step * chunk + block * LANES, LANES), LANES)
            terms[block, 0:81, :] = fc4[:, part].astype(F32)

        def term(start, count, stride=1):
            rows = pl.ds(start, count, stride=stride)
            return jnp.concatenate(
                [terms[block, rows, :] for block in range(chunk // LANES)], 1
            )

        read, write = reads[:, span], writes[:, span]
        read_high = (read >> 7) & 15
        write_high = small((write >> 7) & 15)
        found = jnp.dot(table[...], low_hot(read), preferred_element_type=F32)
        found = found[:144] + found[144:]
        main = found[0:8]
        for high in range(1, 16):
            main = jnp.where(read_high == high, found[8 * high : 8 * high + 8], main)
        last = jnp.sum(jnp.where(level == read_high, found[128:144], 0.0), 0, keepdims=True)
        contrib = term(8, 8, 9) * last
        for comp in range(8):
            contrib = contrib + term(comp, 8, 9) * main[comp : comp + 1]
        ninth = jnp.sum(term(72, 8) * main, 0, keepdims=True) + term(80, 1) * last
        spread = []
        for body, tail in zip(two_parts(contrib), two_parts(ninth)):
            body = jnp.concatenate([body, body], 0).astype(BF16)
            tail = jnp.broadcast_to(tail, level.shape).astype(BF16)
            for pair in range(8):
                spread.append(jnp.where(level_pair + 2 * pair == write_high, body, zero))
            spread.append(jnp.where(level_all == write_high, tail, zero))
        added = lax.dot_general(
            jnp.concatenate(spread, 0),
            low_hot(write),
            (((1,), (1,)), ((), ())),
            preferred_element_type=F32,
        )
        for high in range(2):
            total[high] += added[:, high * LANES : high * LANES + LANES]
        return carry

    lax.fori_loop(0, fc4.shape[1] // chunk, one, 0, unroll=unroll)
    shells = []
    for shell in range(4):
        low, high = shell % 2, shell // 2
        rows = []
        for comp in range(9):
            start = 64 * low + comp if comp < 8 else 128 + 8 * low
            stride = 8 if comp < 8 else 1
            rows.append(
                total[high, pl.ds(start, 8, stride=stride), :]
                + total[high, pl.ds(144 + start, 8, stride=stride), :]
            )
        rows.append(jnp.zeros((LANES - COLS, LANES), F32))
        shells.append(jnp.concatenate(rows, 0).T)
    for j, row in enumerate(pack(shells)):
        out[pl.ds(j, NDEV, stride=OTHER), :] = row


def contract(received, block_in, block_out, fc4, chunk=16384, unroll=1):
    nblocks = fc4.shape[1]
    place = block_tables()
    reads, writes = block_in.reshape(1, nblocks), block_out.reshape(1, nblocks)

    def body(*refs):
        contract_body(chunk, unroll, *refs)

    return pl.pallas_call(
        body,
        out_shape=jax.ShapeDtypeStruct((NDEV * OTHER, LANES), F32),
        scratch_shapes=[
            pltpu.VMEM((4 * COLS, 2 * LANES), BF16),
            pltpu.VMEM((2, 4 * COLS, LANES), F32),
            pltpu.VMEM((chunk // LANES, 88, LANES), F32),
        ],
        compiler_params=params(48),
    )(received, jnp.asarray(place), reads, writes, fc4)


def targets_body(received, shell, target, out):
    rows = []
    for j in range(3):
        piece = received[pl.ds(j, NDEV, stride=OTHER), :]
        rows.append(piece[0:32] + piece[32:64] + piece[64:96] + piece[96:128])
    renorm = jnp.concatenate(unpack(rows), 0)
    source = lax.broadcasted_iota(jnp.int32, (LANES, LANES), 0)
    order = lax.broadcasted_iota(jnp.int32, (LANES, LANES), 1)
    order = jnp.where(source == (order % 32) * 4 + order // 32, 1.0, 0.0)
    pad = jnp.zeros((5, LANES), F32)
    vectors = jnp.concatenate([shell[...].astype(F32), pad], 0)
    points = jnp.concatenate([target[...].astype(F32), pad], 0)
    vectors = jnp.dot(vectors, order, preferred_element_type=F32)
    index = lax.dot_general(
        points, vectors, (((0,), (0,)), ((), ())), preferred_element_type=F32
    )
    out[pl.ds(0, NDEV, stride=2), :] = split_dot(sixteenth_cos(index), renorm)
    out[pl.ds(1, NDEV, stride=2), :] = split_dot(sixteenth_cos(index + 4.0), renorm)


def to_targets(received, shell, target):
    return pl.pallas_call(
        targets_body,
        out_shape=jax.ShapeDtypeStruct((NDEV * 2, LANES), F32),
        compiler_params=params(),
    )(received, shell, target)


def arrange_body(received, out):
    for comp in range(2):
        turned = received[pl.ds(comp, NDEV, stride=2), :].T
        out[pl.ds(comp, COLS, stride=2), :] = turned[:COLS]


def arrange(received):
    rows = pl.pallas_call(
        arrange_body,
        out_shape=jax.ShapeDtypeStruct((2 * COLS, LANES), F32),
        compiler_params=params(),
    )(received)
    rows = rows.reshape(9, NPH, 2, LANES).transpose(2, 0, 1, 3)
    return rows.reshape(1, 2, 9, NPH * LANES)


def exchange(values):
    linear = values.reshape(NDEV, 1, values.size // NDEV)
    return lax.all_to_all(linear, ALL, 0, 0, tiled=True).reshape(values.shape)


def shards(
    modes, occup, qprime_coord, shell_vec, target_coord, pair_atoms, block_in, block_out, fc4
):
    picked = exchange(pick(modes, occup, qprime_coord, pair_atoms))
    density = exchange(to_shells(picked, shell_vec))
    renorm = exchange(contract(density, block_in, block_out, fc4))
    delta = exchange(to_targets(renorm, shell_vec, target_coord))
    return arrange(delta)


def solution(mesh):
    return jax.shard_map(
        shards,
        mesh=mesh,
        in_specs=(
            P(("grp", "slab"), None, None, None),
            P(("grp", "slab"), None),
            P(None, ("grp", "slab")),
            P(),
            P(),
            P(),
            P(("grp", "slab")),
            P(("grp", "slab")),
            P(None, ("grp", "slab")),
        ),
        out_specs=P(("grp", "slab"), None, None, None),
        check_vma=False,
    )
```

```python
import math

import jax
import jax.numpy as jnp
import numpy as np
from jax import lax
from jax.experimental import pallas as pl
from jax.experimental.pallas import tpu as pltpu
from jax.sharding import PartitionSpec as P

MESH = 16
LANES = 128
NDEV = 128
NPH = 8
COLS = 72
PITCH = 4 * 384 + 8
FIRST = 5
OTHER = 3
ALL = ("grp", "slab")
F32 = jnp.float32
BF16 = jnp.bfloat16


def params(mebibytes=40):
    return pltpu.CompilerParams(vmem_limit_bytes=mebibytes * 1024 * 1024)


def sixteenth_cos(index):
    wrapped = index - 16.0 * jnp.floor(index * (1.0 / 16.0))
    folded = 4.0 - jnp.minimum(wrapped, 16.0 - wrapped)
    square = folded * folded
    poly = POLY[3]
    for coefficient in (POLY[2], POLY[1], POLY[0]):
        poly = poly * square + coefficient
    return folded * poly


def odd_polynomial():
    points = np.arange(1, 5, dtype=np.float64)
    values = np.sin(np.pi * points / 8.0)
    powers = np.stack([points ** (2 * k + 1) for k in range(4)], 1)
    return [float(c) for c in np.linalg.solve(powers, values)]


POLY = odd_polynomial()


def pick_body(
    coord, atoms, modes, occup, out, held, weights, pairs, spots, points, scaled, rows, dens, picked, sems
):
    copies = [
        pltpu.make_async_copy(occup, weights, sems.at[4]),
        pltpu.make_async_copy(atoms, pairs, sems.at[5]),
        pltpu.make_async_copy(coord, points, sems.at[6]),
    ]
    loads = [pltpu.make_async_copy(modes.at[q], held.at[q], sems.at[q]) for q in range(4)]
    for copy in copies + loads:
        copy.start()
    copies[1].wait()
    first = pairs[0:1, :]
    second = pairs[1:2, :]
    turn = (128 - 3 * (second & 31)) & 127
    pairs[0:1, :] = ((second >> 5) * 384 + first * 3) * 128 + turn
    move = pltpu.make_async_copy(pairs.at[0], spots, sems.at[7])
    move.start()
    copies[0].wait()
    for q in range(4):
        loads[q].wait()
        weight = weights[q : q + 1, :]
        real, imag = held[q, 0], held[q, 1]
        rows[q % 2, 0:384, 0:384] = real
        rows[q % 2, 0:384, 384:768] = imag
        rows[q % 2, 384:768, 0:384] = imag
        rows[q % 2, 384:768, 384:768] = -real
        for part in range(2):
            values = (held[q, part].astype(F32) * weight).astype(BF16)
            for block in range(4):
                scaled[q % 2, 128 * block : 128 * block + 96, pl.ds(384 * part, 384)] = values[
                    96 * block : 96 * block + 96
                ]
        for comp in range(2):
            for half in range(2):
                tile = lax.dot_general(
                    rows[q % 2, 384 * comp : 384 * comp + 384],
                    scaled[q % 2, 256 * half : 256 * half + 256],
                    (((1,), (1,)), ((), ())),
                    preferred_element_type=F32,
                )
                for low in range(2):
                    base = PITCH * (2 * q + comp) + 384 * (2 * half + low)
                    dens[pl.ds(base, 384), :] = tile[:, 128 * low : 128 * low + 128]

    slot = lax.broadcasted_iota(jnp.int32, (8, LANES), 1) // 3
    copies[2].wait()
    move.wait()

    def one(dev, carry):
        acc = jnp.zeros((8, LANES), F32)
        for high in range(NPH):
            spot = spots[high * LANES + dev]
            base = spot >> 7
            for alpha in range(3):
                low = 24 * alpha + 3 * high
                value = dens[pl.ds(base + alpha, 8, stride=PITCH), :]
                turned = pltpu.roll(value, (spot + low) & 127, 1)
                acc = jnp.where(slot == low // 3, turned, acc)
        picked[pl.ds(pl.multiple_of(8 * dev, 8), 8), :] = acc
        return carry

    lax.fori_loop(0, NDEV, one, 0, unroll=128)
    lane = lax.broadcasted_iota(jnp.int32, (NDEV, LANES), 1)
    parts = [picked[pl.ds(part, NDEV, stride=8), :] for part in range(8)]
    for part in range(4):
        joined = jnp.where(lane < 64, parts[part], pltpu.roll(parts[part + 4], 64, 1))
        out[pl.ds(part, NDEV, stride=FIRST), :] = joined
    column = lax.broadcasted_iota(jnp.int32, (1, LANES), 1)
    last = jnp.zeros((1, LANES), F32)
    for q in range(4):
        for axis in range(3):
            last = jnp.where(column == 64 + 8 * q + axis, points[axis, q].astype(F32), last)
    last = jnp.broadcast_to(last, (NDEV, LANES))
    for part in range(8):
        piece = pltpu.roll(parts[part], (8 * part + 64) % LANES, 1)
        last = jnp.where((lane >= 8 * part) & (lane < 8 * part + 8), piece, last)
    out[pl.ds(4, NDEV, stride=FIRST), :] = last


def pick(modes, occup, coord, atoms):
    anywhere = pl.BlockSpec(memory_space=pltpu.HBM)
    return pl.pallas_call(
        pick_body,
        in_specs=[anywhere] * 4,
        out_specs=pl.BlockSpec(memory_space=pltpu.VMEM),
        out_shape=pltpu.VMEM((NDEV * FIRST, LANES), F32),
        scratch_shapes=[
            pltpu.VMEM((4, 2, 384, 384), BF16),
            pltpu.VMEM((4, 384), F32),
            pltpu.VMEM((2, NPH * LANES), jnp.int32),
            pltpu.SMEM((NPH * LANES,), jnp.int32),
            pltpu.SMEM((3, 4), jnp.int32),
            pltpu.VMEM((2, 512, 768), BF16),
            pltpu.VMEM((2, 768, 768), BF16),
            pltpu.VMEM((PITCH * 9, LANES), F32),
            pltpu.VMEM((8 * NDEV, LANES), F32),
            pltpu.SemaphoreType.DMA((8,)),
        ],
        compiler_params=params(60),
    )(coord, atoms, modes, occup)


def two_parts(values):
    coarse = values.astype(BF16).astype(F32)
    return coarse, values - coarse


def split_dot(left, right):
    left_high, left_low = [part.astype(BF16) for part in two_parts(left)]
    right_high, right_low = [part.astype(BF16) for part in two_parts(right)]
    total = jnp.dot(left_high, right_high, preferred_element_type=F32)
    total = total + jnp.dot(left_high, right_low, preferred_element_type=F32)
    return total + jnp.dot(left_low, right_high, preferred_element_type=F32)


def pack(shells):
    lane = lax.broadcasted_iota(jnp.int32, shells[0].shape, 1)
    return [
        jnp.where(lane < COLS, shells[j], pltpu.roll(shells[3], COLS - 24 * j, 1)) for j in range(3)
    ]


def unpack(rows):
    lane = lax.broadcasted_iota(jnp.int32, rows[0].shape, 1)
    turned = [pltpu.roll(rows[j], LANES - COLS + 24 * j, 1) for j in range(3)]
    last = jnp.where(lane < 24, turned[0], jnp.where(lane < 48, turned[1], turned[2]))
    return [*rows, last]


def shells_body(received, shell, out, summed):
    parts = [received[pl.ds(part, NDEV, stride=FIRST), :] for part in range(FIRST)]
    vector = jnp.concatenate([shell[...].astype(F32), jnp.zeros((5, LANES), F32)], 0)
    vectors = [
        jnp.concatenate(
            [jnp.zeros((64 + 8 * q, LANES), F32), vector, jnp.zeros((56 - 8 * q, LANES), F32)], 0
        )
        for q in range(4)
    ]
    index = lax.dot_general(
        jnp.concatenate(vectors, 1),
        parts[4],
        (((0,), (1,)), ((), ())),
        preferred_element_type=F32,
    )
    waves = [sixteenth_cos(index), sixteenth_cos(index + 4.0)]
    waves = [waves[part % 2][LANES * (part // 2) : LANES * (part // 2 + 1)] for part in range(8)]
    lane = lax.broadcasted_iota(jnp.int32, (NDEV, LANES), 1)
    values = []
    for part in range(8):
        main = parts[part] if part < 4 else pltpu.roll(parts[part - 4], 64, 1)
        rest = pltpu.roll(parts[4], (64 - 8 * part) % LANES, 1)
        values.append(jnp.where(lane < 64, main, rest))
    rho = split_dot(jnp.concatenate(waves, 1), jnp.concatenate(values, 0))
    summed[...] = rho * (1.0 / math.sqrt(512.0))
    rows = pack([summed[pl.ds(low, 32, stride=4), :] for low in range(4)])
    for j in range(3):
        for group in range(4):
            out[pl.ds(OTHER * 32 * group + j, 32, stride=OTHER), :] = rows[j]


def to_shells(received, shell):
    return pl.pallas_call(
        shells_body,
        out_shape=jax.ShapeDtypeStruct((NDEV * OTHER, LANES), F32),
        scratch_shapes=[pltpu.VMEM((LANES, LANES), F32)],
        compiler_params=params(),
    )(received, shell)


def block_tables():
    column = np.arange(2 * COLS)
    rest = column % COLS
    comp = 3 * (rest // 24) + rest % 3
    level = 8 * (column // COLS) + (rest % 24) // 3
    row = np.where(comp < 8, 8 * level + comp, 128 + level)
    return (np.arange(2 * COLS)[:, None] == row[None, :]).astype(np.float32)


def contract_body(
    chunk, unroll, received, place, reads, writes, fc4, out, table, total, terms
):
    shells = unpack([received[pl.ds(j, NDEV, stride=OTHER), :] for j in range(3)])
    for high in range(2):
        pieces = [shells[2 * high + low][:, :COLS] for low in range(2)]
        parts = jnp.concatenate(two_parts(jnp.concatenate(pieces, 1)), 0).astype(BF16)
        turned = lax.dot_general(
            place[...].astype(BF16),
            parts,
            (((1,), (1,)), ((), ())),
            preferred_element_type=F32,
        ).astype(BF16)
        span = pl.ds(high * LANES, LANES)
        table[:, span] = turned[:, :LANES]
        table[:, pl.ds((2 + high) * LANES, LANES)] = turned[:, LANES:]
    total[...] = jnp.zeros_like(total)
    level = lax.broadcasted_iota(jnp.int32, (16, chunk), 0)
    level_pair = (level >> 3).astype(BF16)
    level_all = level.astype(BF16)
    low_place = lax.broadcasted_iota(jnp.int32, (2 * LANES, chunk), 0).astype(BF16)
    unit, zero = jnp.ones((), BF16), jnp.zeros((), BF16)

    def small(values):
        return values.astype(F32).astype(BF16)

    def low_hot(entry):
        low = ((entry >> 11) << 7) | (entry & 127)
        return jnp.where(low_place == small(low), unit, zero)

    def one(step, carry):
        span = pl.ds(pl.multiple_of(step * chunk, chunk), chunk)
        for block in range(chunk // LANES):
            part = pl.ds(pl.multiple_of(step * chunk + block * LANES, LANES), LANES)
            terms[block, 0:81, :] = fc4[:, part].astype(F32)

        def term(start, count, stride=1):
            rows = pl.ds(start, count, stride=stride)
            return jnp.concatenate(
                [terms[block, rows, :] for block in range(chunk // LANES)], 1
            )

        read, write = reads[:, span], writes[:, span]
        read_high = (read >> 7) & 15
        write_high = small((write >> 7) & 15)
        hot = low_hot(read)
        hot = jnp.concatenate([hot, hot], 0)
        found = jnp.dot(table[...], hot, preferred_element_type=F32)
        main = found[0:8]
        for high in range(1, 16):
            main = jnp.where(read_high == high, found[8 * high : 8 * high + 8], main)
        last = jnp.sum(jnp.where(level == read_high, found[128:144], 0.0), 0, keepdims=True)
        contrib = term(8, 8, 9) * last
        for comp in range(8):
            contrib = contrib + term(comp, 8, 9) * main[comp : comp + 1]
        ninth = jnp.sum(term(72, 8) * main, 0, keepdims=True) + term(80, 1) * last
        spread = []
        for body, tail in zip(two_parts(contrib), two_parts(ninth)):
            body = jnp.concatenate([body, body], 0).astype(BF16)
            tail = jnp.broadcast_to(tail, level.shape).astype(BF16)
            for pair in range(8):
                spread.append(jnp.where(level_pair + 2 * pair == write_high, body, zero))
            spread.append(jnp.where(level_all == write_high, tail, zero))
        added = lax.dot_general(
            jnp.concatenate(spread, 0),
            low_hot(write),
            (((1,), (1,)), ((), ())),
            preferred_element_type=F32,
        )
        for high in range(2):
            total[high] += added[:, high * LANES : high * LANES + LANES]
        return carry

    lax.fori_loop(0, fc4.shape[1] // chunk, one, 0, unroll=unroll)
    shells = []
    for shell in range(4):
        low, high = shell % 2, shell // 2
        rows = []
        for comp in range(9):
            start = 64 * low + comp if comp < 8 else 128 + 8 * low
            stride = 8 if comp < 8 else 1
            rows.append(
                total[high, pl.ds(start, 8, stride=stride), :]
                + total[high, pl.ds(144 + start, 8, stride=stride), :]
            )
        rows.append(jnp.zeros((LANES - COLS, LANES), F32))
        shells.append(jnp.concatenate(rows, 0).T)
    for j, row in enumerate(pack(shells)):
        out[pl.ds(j, NDEV, stride=OTHER), :] = row


def contract(received, block_in, block_out, fc4, chunk=16384, unroll=1):
    nblocks = fc4.shape[1]
    place = block_tables()
    reads, writes = block_in.reshape(1, nblocks), block_out.reshape(1, nblocks)

    def body(*refs):
        contract_body(chunk, unroll, *refs)

    return pl.pallas_call(
        body,
        out_shape=jax.ShapeDtypeStruct((NDEV * OTHER, LANES), F32),
        scratch_shapes=[
            pltpu.VMEM((2 * COLS, 4 * LANES), BF16),
            pltpu.VMEM((2, 4 * COLS, LANES), F32),
            pltpu.VMEM((chunk // LANES, 88, LANES), F32),
        ],
        compiler_params=params(48),
    )(received, jnp.asarray(place), reads, writes, fc4)


def targets_body(received, shell, target, out):
    rows = []
    for j in range(3):
        piece = received[pl.ds(j, NDEV, stride=OTHER), :]
        rows.append(piece[0:32] + piece[32:64] + piece[64:96] + piece[96:128])
    renorm = jnp.concatenate(unpack(rows), 0)
    source = lax.broadcasted_iota(jnp.int32, (LANES, LANES), 0)
    order = lax.broadcasted_iota(jnp.int32, (LANES, LANES), 1)
    order = jnp.where(source == (order % 32) * 4 + order // 32, 1.0, 0.0)
    pad = jnp.zeros((5, LANES), F32)
    vectors = jnp.concatenate([shell[...].astype(F32), pad], 0)
    points = jnp.concatenate([target[...].astype(F32), pad], 0)
    vectors = jnp.dot(vectors, order, preferred_element_type=F32)
    index = lax.dot_general(
        points, vectors, (((0,), (0,)), ((), ())), preferred_element_type=F32
    )
    out[pl.ds(0, NDEV, stride=2), :] = split_dot(sixteenth_cos(index), renorm)
    out[pl.ds(1, NDEV, stride=2), :] = split_dot(sixteenth_cos(index + 4.0), renorm)


def to_targets(received, shell, target):
    return pl.pallas_call(
        targets_body,
        out_shape=jax.ShapeDtypeStruct((NDEV * 2, LANES), F32),
        compiler_params=params(),
    )(received, shell, target)


def arrange_body(received, out):
    for comp in range(2):
        turned = received[pl.ds(comp, NDEV, stride=2), :].T
        out[pl.ds(comp, COLS, stride=2), :] = turned[:COLS]


def arrange(received):
    rows = pl.pallas_call(
        arrange_body,
        out_shape=jax.ShapeDtypeStruct((2 * COLS, LANES), F32),
        compiler_params=params(),
    )(received)
    rows = rows.reshape(9, NPH, 2, LANES).transpose(2, 0, 1, 3)
    return rows.reshape(1, 2, 9, NPH * LANES)


def exchange(values):
    linear = values.reshape(NDEV, 1, values.size // NDEV)
    return lax.all_to_all(linear, ALL, 0, 0, tiled=True).reshape(values.shape)


def shards(
    modes, occup, qprime_coord, shell_vec, target_coord, pair_atoms, block_in, block_out, fc4
):
    picked = exchange(pick(modes, occup, qprime_coord, pair_atoms))
    density = exchange(to_shells(picked, shell_vec))
    renorm = exchange(contract(density, block_in, block_out, fc4))
    delta = exchange(to_targets(renorm, shell_vec, target_coord))
    return arrange(delta)


def solution(mesh):
    return jax.shard_map(
        shards,
        mesh=mesh,
        in_specs=(
            P(("grp", "slab"), None, None, None),
            P(("grp", "slab"), None),
            P(None, ("grp", "slab")),
            P(),
            P(),
            P(),
            P(("grp", "slab")),
            P(("grp", "slab")),
            P(None, ("grp", "slab")),
        ),
        out_specs=P(("grp", "slab"), None, None, None),
        check_vma=False,
    )
```
